32 devices in a mesh: replica: 4 (over z), tensor: 4 (over y, x), section: 2 (over core).
Axes of the slice: x: 2, y: 2, z: 4, core: 2. Of those that a mesh axis runs over, the one named last changes fastest.
Arguments:
- grads: bfloat16 [4, 2, 1024, 1024], P('replica', 'section', None, 'tensor'), may hold values from -250 to 250
- errors: bfloat16 [4, 2, 1024, 1024], P('replica', 'section', None, 'tensor'), may hold values from -3 to 3
- q_start: float32 [2, 1024, 32], P('section', 'tensor'), may hold values from -6 to 6
- momentum: float32 [2, 1024, 1024], P('section', 'replica', 'tensor'), may hold values from -6 to 6
- vec_grads: float32 [4, 2, 1024], P('replica', 'section', 'tensor'), may hold values from -6 to 6
- vec_momentum: float32 [2, 1024], P('section', 'tensor'), may hold values from -6 to 6
Outputs:
- new_errors: bfloat16 [4, 2, 1024, 1024], P('replica', 'section', None, 'tensor')
- new_momentum: float32 [2, 1024, 1024], P('section', 'replica', 'tensor')
- new_vec_momentum: float32 [2, 1024], P('section', 'tensor')
The draws below stay inside these ranges and needn't reach their ends.
All inputs are finite; a program needn't handle non-finite values.
Results may differ from the reference program's by a relative error of at most 0.0034.
The reference program's roundings to bfloat16 on the way (of `merged`, `q_lo` and `p_lo`) count: a program that leaves them out, or rounds other values in their place, can miss the bound.
Values may be sent and summed in bfloat16 or wider, within the bound.
No kernel may reach another device: no remote copies, remote signals or barrier semaphores. Data moves between devices by JAX's collectives and lax.ppermute only.
A program may use at most 64 MiB of HBM per device.

```python
import jax
import jax.numpy as jnp
from jax import lax

D = 1024
RANK = 32
ROUNDS = 2
NB = 2
COLS = 1024
N_REPLICA = 4


def draw_grads(key, part):
    key_one = jax.random.fold_in(key, 11)
    key_two = jax.random.fold_in(key, 12)
    key_three = jax.random.fold_in(key, 13)
    key_four = jax.random.fold_in(key, 14)
    full_shape = (N_REPLICA, NB, D, D)
    row_part = jax.random.normal(key_one, (1, NB, D, 1), jnp.float32)
    col_part = jax.random.normal(key_two, (1, NB, 1, D), jnp.float32)
    common = 0.6 * jax.random.normal(key_three, (1, NB, D, D), jnp.float32) + 0.15 * row_part * col_part
    own_part = jax.random.normal(key_four, full_shape, jnp.float32)
    row_block = jnp.arange(D) // (D // N_REPLICA)
    replica_ids = jnp.arange(N_REPLICA)
    lift_rows = jnp.where(row_block[None, None, :, None] == replica_ids[:, None, None, None], 4.0, 1.0)
    values = common + 0.5 * own_part * lift_rows
    return jnp.clip(values, -250.0, 250.0).astype(jnp.bfloat16)


def steps_of(stream_key, dims, cuts, low, top_value):
    loudness = 1.0
    for position, blocks in cuts:
        heights = jax.random.uniform(jax.random.fold_in(jax.random.fold_in(stream_key, 6), position), (blocks,), jnp.float32, low / len(cuts), top_value / len(cuts))
        loudness = loudness * jnp.repeat(jnp.exp(heights), dims[position] // blocks).reshape((-1,) + (1,) * (len(dims) - 1 - position))
    return loudness


def bell_draw(own_key, shape, width, reach, split=(), held_as=jnp.bfloat16):
    array = jax.random.normal(own_key, shape, jnp.float32) * width
    if len(split) > 0:
        array = steps_of(own_key, shape, split, -0.22, 0.18) * array
    return jnp.clip(array, min=-reach, max=reach).astype(held_as)


def setup_inputs(seed: int = 0) -> dict:
    seeds = jax.random.split(jax.random.key(seed), 7)
    grads = draw_grads(jax.random.fold_in(seeds[6], 71), 0)
    errors = bell_draw(seeds[1], (N_REPLICA, NB, D, COLS), 0.5, 3.0, ((0, 4), (1, 2), (3, 4)))
    q_start = bell_draw(seeds[2], (NB, COLS, RANK), 1.0, 6.0, ((0, 2), (1, 4)), jnp.float32)
    momentum = bell_draw(seeds[3], (NB, D, COLS), 1.0, 6.0, ((0, 2), (1, 4), (2, 4)), jnp.float32)
    vec_grads = bell_draw(seeds[4], (N_REPLICA, NB, COLS), 1.0, 6.0, ((0, 4), (1, 2), (2, 4)), jnp.float32)
    vec_momentum = bell_draw(seeds[5], (NB, COLS), 1.0, 6.0, ((0, 2), (1, 4)), jnp.float32)
    return {"grads": grads, "errors": errors, "q_start": q_start, "momentum": momentum, "vec_grads": vec_grads, "vec_momentum": vec_momentum}


def merge_pair(grad_one, error_one):
    return (grad_one.astype(jnp.float32) + error_one.astype(jnp.float32)).astype(jnp.bfloat16)

def orthonormal(p_sum):
    gram_mat = jnp.einsum('bdr,bds->brs', p_sum, p_sum, precision=lax.Precision.HIGHEST)
    factor = jnp.linalg.cholesky(gram_mat)

    def solve_one(lower, matrix):
        return jax.scipy.linalg.solve_triangular(lower, matrix.T, lower=True).T
    return jax.vmap(solve_one)(factor, p_sum)

def reference(grads, errors, q_start, momentum, vec_grads, vec_momentum):
    q_lo = q_start.astype(jnp.bfloat16)
    p_lo = None
    for round_no in range(ROUNDS):

        def add_left(total, pieces):
            merged = merge_pair(pieces[0], pieces[1])
            return (total + jnp.einsum('bdc,bcr->bdr', merged.astype(jnp.float32), q_lo.astype(jnp.float32)), None)
        p_zero = jnp.zeros((NB, D, RANK), jnp.float32)
        p_sum = lax.scan(add_left, p_zero, (grads, errors))[0] / N_REPLICA
        p_lo = orthonormal(p_sum).astype(jnp.bfloat16)

        def add_right(total, pieces):
            merged = merge_pair(pieces[0], pieces[1])
            return (total + jnp.einsum('bdc,bdr->bcr', merged.astype(jnp.float32), p_lo.astype(jnp.float32)), None)
        q_zero = jnp.zeros((NB, COLS, RANK), jnp.float32)
        q_sum = lax.scan(add_right, q_zero, (grads, errors))[0] / N_REPLICA
        q_lo = q_sum.astype(jnp.bfloat16)
    approx = jnp.einsum('bdr,bcr->bdc', p_lo.astype(jnp.float32), q_lo.astype(jnp.float32))

    def error_one(pieces):
        merged = merge_pair(pieces[0], pieces[1])
        return (merged.astype(jnp.float32) - approx).astype(jnp.bfloat16)
    new_errors = lax.map(error_one, (grads, errors))
    new_momentum = 0.9 * momentum + approx
    new_vec_momentum = 0.9 * vec_momentum + jnp.sum(vec_grads, axis=0) / N_REPLICA
    return (new_errors, new_momentum, new_vec_momentum)
```

```python
import functools

import jax
import jax.numpy as jnp
from jax import lax
from jax.experimental import pallas as pl
from jax.experimental.pallas import tpu as pltpu
from jax.sharding import PartitionSpec as P

ROUNDS = 2
GATHER_MAX = 8
PAD = 16
STEP = 8
HIGHEST = lax.Precision.HIGHEST
F32, BF16 = jnp.float32, jnp.bfloat16
VMEM = pl.BlockSpec(memory_space=pltpu.VMEM)


def dot(a, b, ca, cb, precision=None):
    return lax.dot_general(a, b, (((ca,), (cb,)), ((), ())), precision=precision, preferred_element_type=F32)


def call(kernel, outs, *args, flops=0, scratch=()):
    size = sum(a.size * a.dtype.itemsize for a in (*args, *outs))
    return pl.pallas_call(
        kernel,
        out_shape=outs,
        in_specs=[VMEM] * len(args),
        out_specs=[VMEM] * len(outs),
        scratch_shapes=scratch,
        compiler_params=pltpu.CompilerParams(vmem_limit_bytes=32 * 1024 * 1024),
        cost_estimate=pl.CostEstimate(flops=flops, bytes_accessed=size, transcendentals=0),
    )(*args)


def three_parts(x):
    hi = x.astype(BF16).astype(F32)
    mid = (x - hi).astype(BF16).astype(F32)
    lo = (x - hi - mid).astype(BF16).astype(F32)
    return hi, mid, lo


def tree(values):
    values = list(values)
    while len(values) > 1:
        values = [a + b for a, b in zip(values[::2], values[1::2])] + values[len(values) & ~1 :]
    return values[0]


def inverse_factor(gram):
    n = gram.shape[0]
    wide = max(128, 2 * n)
    eye = (lax.broadcasted_iota(jnp.int32, (n, n), 0) == lax.broadcasted_iota(jnp.int32, (n, n), 1)).astype(F32)
    row = lax.broadcasted_iota(jnp.int32, (n, wide), 0)
    both = jnp.concatenate([gram, eye, jnp.zeros((n, wide - 2 * n), F32)], axis=1)
    scale = jnp.zeros((n, wide), F32)
    for first in range(0, n, STEP):
        columns = [jnp.broadcast_to(both[:, k : k + 1], (n, wide)) for k in range(first, first + STEP)]
        for j in range(STEP):
            k = first + j
            inverse = 1.0 / jnp.broadcast_to(columns[j][k : k + 1, :], (n, wide))
            scale = jnp.where(row == k, inverse, scale)
            factor = jnp.where(row > k, columns[j] * inverse, 0.0)
            for i in range(j + 1, STEP):
                columns[i] = columns[i] - factor * columns[i][k : k + 1, :]
            both = both - factor * both[k : k + 1, :]
    return both[:, n : 2 * n] * jnp.sqrt(scale[:, :n])


def merge_kernel(grads, errors, q, vec, merged, p_part):
    rows, cols = grads.shape
    total = (grads[...].astype(F32) + errors[...].astype(F32)).astype(BF16)
    merged[:rows, :] = total
    parts = three_parts(vec[...])
    merged[rows:, :] = jnp.concatenate([*parts, jnp.zeros((PAD - 3, cols), F32)], axis=0).astype(BF16)
    p_part[...] = dot(q[...].T.astype(BF16), total, 1, 1)


def add_kernel(*refs):
    refs[-1][...] = tree([r[...] for r in refs[:-1]])


def factor_kernel(n_p, replicas, last, *refs):
    p_parts, merged, out = refs[:n_p], refs[n_p:-1], refs[-1]
    rows, cols = merged[0].shape[0] - PAD, merged[0].shape[1]
    p_sum = tree([p[...] for p in p_parts]) * (1.0 / replicas)
    inverse = inverse_factor(dot(p_sum, p_sum, 1, 1, HIGHEST))
    p_lo = dot(inverse, p_sum, 1, 0, HIGHEST).astype(BF16)
    q_sum = tree([dot(p_lo, m[:rows, :], 1, 0) for m in merged])
    q_lo = (q_sum * (1.0 / replicas)).astype(BF16)
    if not last:
        out[...] = tree([dot(q_lo, m[:rows, :], 1, 1) for m in merged])
        return
    out[:, :rows] = p_lo
    out[:, rows : rows + cols] = q_lo
    vec = tree([jnp.sum(m[rows:, :].astype(F32), axis=0, keepdims=True) for m in merged]) * (1.0 / replicas)
    parts = three_parts(vec)
    out[:, rows + cols :] = jnp.concatenate([*parts, jnp.zeros((out.shape[0] - 3, cols), F32)], axis=0).astype(BF16)


def final_kernel(owners, *refs):
    place, own, *received = refs[: -9]
    merged, momentum, vec_momentum, new_errors, new_momentum, new_vec, pack, p_rows, unused = refs[-9:]
    del unused
    rows, cols = new_errors.shape
    own_rows = momentum.shape[0]
    is_owner = place[1] == 1

    @pl.when(is_owner)
    def _():
        pack[...] = own[...]

    @pl.when(jnp.logical_not(is_owner))
    def _():
        pack[...] = sum(r[...].astype(F32) for r in received).astype(BF16)

    p_rows[...] = pack[:, :rows].T
    q_lo = pack[:, rows : rows + cols]
    approx = dot(p_rows[...], q_lo, 1, 0)
    new_errors[...] = (merged[:rows, :].astype(F32) - approx).astype(BF16)
    first = pl.multiple_of(place[0] * own_rows, own_rows)
    mine = dot(p_rows[pl.ds(first, own_rows), :], q_lo, 1, 0)
    new_momentum[...] = 0.9 * momentum[...] + mine
    vec = jnp.sum(pack[:, rows + cols :].astype(F32), axis=0, keepdims=True)
    new_vec[...] = 0.9 * vec_momentum[...] + vec


def gathered(grads, errors, q_start, momentum, vec_grads, vec_momentum):
    replicas, tensors, sections = (lax.axis_size(a) for a in ("replica", "tensor", "section"))
    rows, cols = grads.shape[2:]
    rank = q_start.shape[2]
    middle = (replicas - 1) // 2
    owner = [middle + s % min(2, replicas) for s in range(sections)]
    sources = [sorted((z for z in range(replicas) if z != o), key=lambda z, o=o: -abs(z - o)) for o in owner]
    inward = [
        [(sources[s][j] * sections + s, owner[s] * sections + s) for s in range(sections)] for j in range(replicas - 1)
    ]
    outward = [[(b, a) for a, b in pairs] for pairs in inward]

    def along(x, perms):
        return [lax.ppermute(x, ("replica", "section"), p) for p in perms]

    def across(x):
        return [x] + [lax.ppermute(x, "tensor", [(i, i ^ k) for i in range(tensors)]) for k in range(1, tensors)]

    p_shape = jax.ShapeDtypeStruct((rank, rows), F32)
    work = 2 * rows * cols * rank
    merged, p_part = call(
        merge_kernel,
        [jax.ShapeDtypeStruct((rows + PAD, cols), BF16), p_shape],
        grads[0, 0],
        errors[0, 0],
        q_start[0],
        vec_grads[0],
        flops=work,
    )
    p_in = along(p_part, inward)
    m_in = along(merged, inward)
    p_part = call(add_kernel, [p_shape], p_part, *p_in)[0]
    for round_no in range(ROUNDS):
        last = round_no == ROUNDS - 1
        shape = jax.ShapeDtypeStruct((rank, rows + 2 * cols), BF16) if last else p_shape
        parts = across(p_part)
        p_part = call(
            functools.partial(factor_kernel, len(parts), replicas, last),
            [shape],
            *parts,
            merged,
            *m_in,
            flops=2 * replicas * work,
        )[0]
    received = along(p_part, outward)
    z, s = lax.axis_index("replica"), lax.axis_index("section")
    place = jnp.stack([z, (z == jnp.asarray(owner)[s]).astype(jnp.int32)])
    outs = [
        jax.ShapeDtypeStruct((rows, cols), BF16),
        jax.ShapeDtypeStruct(momentum.shape[1:], F32),
        jax.ShapeDtypeStruct((1, cols), F32),
    ]
    args = [place, p_part, *received, merged, momentum[0], vec_momentum]
    errors_out, momentum_out, vec_out = pl.pallas_call(
        functools.partial(final_kernel, owner),
        out_shape=outs,
        in_specs=[pl.BlockSpec(memory_space=pltpu.SMEM)] + [VMEM] * (len(args) - 1),
        out_specs=[VMEM] * 3,
        scratch_shapes=[
            pltpu.VMEM(p_part.shape, BF16),
            pltpu.VMEM((rows, rank), BF16),
            pltpu.VMEM((8, 128), F32),
        ],
        compiler_params=pltpu.CompilerParams(vmem_limit_bytes=32 * 1024 * 1024),
    )(*args)
    return errors_out[None, None], momentum_out[None], vec_out


def reduced(grads, errors, q_start, momentum, vec_grads, vec_momentum):
    replicas = lax.axis_size("replica")
    merged = (grads[0].astype(F32) + errors[0].astype(F32)).astype(BF16)
    q_lo = q_start.astype(BF16)
    vec_sum = lax.psum(vec_grads[0], "replica")
    p_lo = None
    for _ in range(ROUNDS):
        p_part = jnp.einsum("bdc,bcr->brd", merged, q_lo, preferred_element_type=F32)
        p_sum = lax.psum(p_part, ("replica", "tensor")) / replicas
        gram = jnp.einsum("brd,bsd->brs", p_sum, p_sum, precision=HIGHEST)
        inverse = jnp.stack([inverse_factor(g) for g in gram])
        p_lo = jnp.einsum("brs,bsd->brd", inverse, p_sum, precision=HIGHEST).astype(BF16)
        q_part = jnp.einsum("bdc,brd->bcr", merged, p_lo, preferred_element_type=F32)
        q_lo = (lax.psum(q_part, "replica") / replicas).astype(BF16)
    approx = jnp.einsum("brd,bcr->bdc", p_lo, q_lo, preferred_element_type=F32)
    new_errors = (merged.astype(F32) - approx).astype(BF16)[None]
    own_rows = momentum.shape[1]
    mine = lax.dynamic_slice_in_dim(approx, lax.axis_index("replica") * own_rows, own_rows, 1)
    return new_errors, 0.9 * momentum + mine, 0.9 * vec_momentum + vec_sum / replicas


def solution(mesh):
    few = mesh.shape["replica"] <= GATHER_MAX
    wide = P("replica", "section", None, "tensor")
    outs = (wide, P("section", "replica", "tensor"), P("section", "tensor"))
    return jax.shard_map(
        gathered if few else reduced,
        mesh=mesh,
        in_specs=(wide, wide, P("section", "tensor", None), outs[1], P("replica", "section", "tensor"), outs[2]),
        out_specs=outs,
        check_vma=False,
    )
```

```python
import functools

import jax
import jax.numpy as jnp
from jax import lax
from jax.experimental import pallas as pl
from jax.experimental.pallas import tpu as pltpu
from jax.sharding import PartitionSpec as P

ROUNDS = 2
GATHER_MAX = 8
PAD = 16
CHUNKS = 4
STEP = 8
HIGHEST = lax.Precision.HIGHEST
F32, BF16 = jnp.float32, jnp.bfloat16
VMEM = pl.BlockSpec(memory_space=pltpu.VMEM)
HBM = pl.BlockSpec(memory_space=pltpu.MemorySpace.HBM)


def dot(a, b, ca, cb, precision=None):
    return lax.dot_general(a, b, (((ca,), (cb,)), ((), ())), precision=precision, preferred_element_type=F32)


def call(kernel, outs, *args, flops=0, in_specs=None, out_specs=None, scratch=(), limit=32, cost=None):
    size = sum(a.size * a.dtype.itemsize for a in (*args, *outs))
    return pl.pallas_call(
        kernel,
        out_shape=outs,
        in_specs=in_specs or [VMEM] * len(args),
        out_specs=out_specs or [VMEM] * len(outs),
        scratch_shapes=scratch,
        compiler_params=pltpu.CompilerParams(vmem_limit_bytes=limit * 1024 * 1024),
        cost_estimate=pl.CostEstimate(flops=flops, bytes_accessed=cost or size, transcendentals=0),
    )(*args)


def three_parts(x):
    hi = x.astype(BF16).astype(F32)
    mid = (x - hi).astype(BF16).astype(F32)
    lo = (x - hi - mid).astype(BF16).astype(F32)
    return hi, mid, lo


def tree(values):
    values = list(values)
    while len(values) > 1:
        values = [a + b for a, b in zip(values[::2], values[1::2])] + values[len(values) & ~1 :]
    return values[0]


def inverse_factor(gram):
    n = gram.shape[0]
    wide = max(128, 2 * n)
    eye = (lax.broadcasted_iota(jnp.int32, (n, n), 0) == lax.broadcasted_iota(jnp.int32, (n, n), 1)).astype(F32)
    row = lax.broadcasted_iota(jnp.int32, (n, wide), 0)
    both = jnp.concatenate([gram, eye, jnp.zeros((n, wide - 2 * n), F32)], axis=1)
    scale = jnp.zeros((n, wide), F32)
    for first in range(0, n, STEP):
        columns = [jnp.broadcast_to(both[:, k : k + 1], (n, wide)) for k in range(first, first + STEP)]
        for j in range(STEP):
            k = first + j
            inverse = 1.0 / jnp.broadcast_to(columns[j][k : k + 1, :], (n, wide))
            scale = jnp.where(row == k, inverse, scale)
            factor = jnp.where(row > k, columns[j] * inverse, 0.0)
            for i in range(j + 1, STEP):
                columns[i] = columns[i] - factor * columns[i][k : k + 1, :]
            both = both - factor * both[k : k + 1, :]
    return both[:, n : 2 * n] * jnp.sqrt(scale[:, :n])


def merge_kernel(grads, errors, q, vec, merged, p_part, grads_in, errors_in, q_in, vec_in, sems):
    rows, cols = grads.shape
    step = rows // CHUNKS
    small = [pltpu.make_async_copy(a, b, sems.at[2, i]) for i, (a, b) in enumerate([(q, q_in), (vec, vec_in)])]
    large = [
        [
            pltpu.make_async_copy(a.at[pl.ds(i * step, step)], b.at[pl.ds(i * step, step)], sems.at[j, i])
            for j, (a, b) in enumerate([(grads, grads_in), (errors, errors_in)])
        ]
        for i in range(CHUNKS)
    ]
    for copy in small + sum(large, []):
        copy.start()
    for copy in small:
        copy.wait()
    q_lo = q_in[...].astype(BF16)
    parts = three_parts(vec_in[...])
    merged[rows:, :] = jnp.concatenate([*parts, jnp.zeros((PAD - 3, cols), F32)], axis=0).astype(BF16)
    for i in range(CHUNKS):
        for copy in large[i]:
            copy.wait()
        here = slice(i * step, (i + 1) * step)
        total = (grads_in[here, :].astype(F32) + errors_in[here, :].astype(F32)).astype(BF16)
        merged[here, :] = total
        p_part[:, here] = dot(q_lo, total, 1, 1)


def add_kernel(*refs):
    refs[-1][...] = tree([r[...] for r in refs[:-1]])


def factor_kernel(n_p, replicas, last, *refs):
    p_parts, merged, out = refs[:n_p], refs[n_p:-1], refs[-1]
    rows, cols = merged[0].shape[0] - PAD, merged[0].shape[1]
    p_sum = tree([p[...] for p in p_parts]) * (1.0 / replicas)
    inverse = inverse_factor(dot(p_sum, p_sum, 1, 1, HIGHEST))
    p_lo = dot(inverse, p_sum, 1, 0, HIGHEST).astype(BF16)
    q_sum = tree([dot(p_lo, m[:rows, :], 1, 0) for m in merged])
    q_lo = (q_sum * (1.0 / replicas)).astype(BF16)
    if not last:
        out[...] = tree([dot(q_lo, m[:rows, :], 1, 1) for m in merged])
        return
    out[:, :rows] = p_lo
    out[:, rows : rows + cols] = q_lo
    vec = tree([jnp.sum(m[rows:, :].astype(F32), axis=0, keepdims=True) for m in merged]) * (1.0 / replicas)
    parts = three_parts(vec)
    out[:, rows + cols :] = jnp.concatenate([*parts, jnp.zeros((out.shape[0] - 3, cols), F32)], axis=0).astype(BF16)


def final_kernel(place, merged, momentum, vec_momentum, *refs):
    packs = refs[:-9]
    new_errors, new_momentum, new_vec, pack, p_rows, errors_out, momentum_out, vec_out, sems = refs[-9:]
    rows, cols = new_errors.shape
    own_rows = momentum.shape[0]
    for i, candidate in enumerate(packs):

        @pl.when(place[1] == i)
        def _(candidate=candidate):
            pack[...] = candidate[...]

    p_rows[...] = pack[:, :rows].T
    q_lo = pack[:, rows : rows + cols]
    copies = []
    step = rows // CHUNKS
    for i in range(CHUNKS):
        here = pl.ds(i * step, step)
        approx = dot(p_rows[here, :], q_lo, 1, 0)
        errors_out[here, :] = (merged[here, :].astype(F32) - approx).astype(BF16)
        copies.append(pltpu.make_async_copy(errors_out.at[here], new_errors.at[here], sems.at[i]))
        copies[-1].start()
    first = pl.multiple_of(place[0] * own_rows, own_rows)
    mine = dot(p_rows[pl.ds(first, own_rows), :], q_lo, 1, 0)
    momentum_out[...] = 0.9 * momentum[...] + mine
    copies.append(pltpu.make_async_copy(momentum_out, new_momentum, sems.at[CHUNKS]))
    copies[-1].start()
    vec = jnp.sum(pack[:, rows + cols :].astype(F32), axis=0, keepdims=True)
    vec_out[...] = 0.9 * vec_momentum[...] + vec
    copies.append(pltpu.make_async_copy(vec_out, new_vec, sems.at[CHUNKS + 1]))
    copies[-1].start()
    for copy in copies:
        copy.wait()


def completed(needed, places):
    needed = list(needed)
    sources = [p for p in places if p not in [a for a, _ in needed]]
    targets = [p for p in places if p not in [b for _, b in needed]]
    far = {(a, b): (a == b, 2 * abs(a[0] - b[0]) + (a[1] != b[1]), a, b) for a in sources for b in targets}
    for a, b in sorted(far, key=far.get):
        if a in sources and b in targets:
            sources.remove(a)
            targets.remove(b)
            needed.append((a, b))
    return needed


def gathered(grads, errors, q_start, momentum, vec_grads, vec_momentum):
    replicas, tensors, sections = (lax.axis_size(a) for a in ("replica", "tensor", "section"))
    rows, cols = grads.shape[2:]
    rank = q_start.shape[2]
    middle = (replicas - 1) // 2
    owner = [middle + s % min(2, replicas) for s in range(sections)]
    sources = [sorted((z for z in range(replicas) if z != o), key=lambda z, o=o: (-abs(z - o), abs(2 * z - replicas + 1))) for o in owner]
    places = [(z, s) for z in range(replicas) for s in range(sections)]
    inward = [
        completed([((sources[s][j], s), (owner[s], s)) for s in range(sections)], places) for j in range(replicas - 1)
    ]
    outward = [[(b, a) for a, b in pairs] for pairs in inward]
    number = lambda place: place[0] * sections + place[1]

    def along(x, perms):
        return [lax.ppermute(x, ("replica", "section"), [(number(a), number(b)) for a, b in p]) for p in perms]

    def across(x, hold):
        parts = [x]
        for k in range(1, tensors):
            if k == tensors - 1 and hold is not None:
                x = lax.optimization_barrier((x, hold))[0]
            needed = [((owner[s], i, s), (owner[s], i ^ k, s)) for s in range(sections) for i in range(tensors)]
            idle = [p for p in places if p[0] != owner[p[1]]]
            pairs = needed + [((a[0], i, a[1]), (b[0], i, b[1])) for a, b in completed([], idle) for i in range(tensors)]
            order = [((a[0] * tensors + a[1]) * sections + a[2], (b[0] * tensors + b[1]) * sections + b[2]) for a, b in pairs]
            parts.append(lax.ppermute(x, ("replica", "tensor", "section"), order))
        return parts

    p_shape = jax.ShapeDtypeStruct((rank, rows), F32)
    work = 2 * rows * cols * rank
    block = (rows, cols)
    merged_shape = jax.ShapeDtypeStruct((rows + PAD, cols), BF16)
    merged, p_part = call(
        merge_kernel,
        [merged_shape, p_shape],
        grads[0, 0],
        errors[0, 0],
        q_start[0].T,
        vec_grads[0],
        flops=work,
        in_specs=[HBM] * 4, limit=60,
        scratch=[
            pltpu.VMEM(block, BF16),
            pltpu.VMEM(block, BF16),
            pltpu.VMEM((rank, cols), F32),
            pltpu.VMEM((1, cols), F32),
            pltpu.SemaphoreType.DMA((3, CHUNKS)),
        ],
    )
    p_in = along(p_part, inward)
    m_near = along(merged, inward[1:])
    p_part = call(add_kernel, [p_shape], p_part, *p_in)[0]
    held = lax.optimization_barrier((merged, p_part))[0]
    m_in = along(held, inward[:1]) + m_near
    for round_no in range(ROUNDS):
        last = round_no == ROUNDS - 1
        shape = jax.ShapeDtypeStruct((rank, rows + 2 * cols), BF16) if last else p_shape
        parts = across(p_part, None if round_no else m_in[-1])
        p_part = call(
            functools.partial(factor_kernel, len(parts), replicas, last),
            [shape],
            *parts,
            merged,
            *m_in,
            flops=2 * replicas * work,
        )[0]
    received = along(p_part, outward)
    z, s = lax.axis_index("replica"), lax.axis_index("section")
    came = sum(
        jnp.where((z == sources[i][j]) & (s == i), j + 1, 0) for i in range(sections) for j in range(replicas - 1)
    )
    new_errors, new_momentum, new_vec = call(
        final_kernel,
        [
            jax.ShapeDtypeStruct(block, BF16),
            jax.ShapeDtypeStruct(momentum.shape[1:], F32),
            jax.ShapeDtypeStruct((1, cols), F32),
        ],
        jnp.stack([z, came]).astype(jnp.int32),
        merged,
        momentum[0],
        vec_momentum,
        p_part,
        *received,
        flops=2 * work,
        in_specs=[pl.BlockSpec(memory_space=pltpu.SMEM)] + [VMEM] * (replicas + 3),
        out_specs=[HBM] * 3,
        scratch=[
            pltpu.VMEM(p_part.shape, BF16),
            pltpu.VMEM((rows, rank), BF16),
            pltpu.VMEM(block, BF16),
            pltpu.VMEM(momentum.shape[1:], F32),
            pltpu.VMEM((1, cols), F32),
            pltpu.SemaphoreType.DMA((CHUNKS + 2,)),
        ],
    )
    return new_errors[None, None], new_momentum[None], new_vec


def reduced(grads, errors, q_start, momentum, vec_grads, vec_momentum):
    replicas = lax.axis_size("replica")
    merged = (grads[0].astype(F32) + errors[0].astype(F32)).astype(BF16)
    q_lo = q_start.astype(BF16)
    vec_sum = lax.psum(vec_grads[0], "replica")
    p_lo = None
    for _ in range(ROUNDS):
        p_part = jnp.einsum("bdc,bcr->brd", merged, q_lo, preferred_element_type=F32)
        p_sum = lax.psum(p_part, ("replica", "tensor")) / replicas
        gram = jnp.einsum("brd,bsd->brs", p_sum, p_sum, precision=HIGHEST)
        inverse = jnp.stack([inverse_factor(g) for g in gram])
        p_lo = jnp.einsum("brs,bsd->brd", inverse, p_sum, precision=HIGHEST).astype(BF16)
        q_part = jnp.einsum("bdc,brd->bcr", merged, p_lo, preferred_element_type=F32)
        q_lo = (lax.psum(q_part, "replica") / replicas).astype(BF16)
    approx = jnp.einsum("brd,bcr->bdc", p_lo, q_lo, preferred_element_type=F32)
    new_errors = (merged.astype(F32) - approx).astype(BF16)[None]
    own_rows = momentum.shape[1]
    mine = lax.dynamic_slice_in_dim(approx, lax.axis_index("replica") * own_rows, own_rows, 1)
    return new_errors, 0.9 * momentum + mine, 0.9 * vec_momentum + vec_sum / replicas


def solution(mesh):
    few = mesh.shape["replica"] <= GATHER_MAX
    wide = P("replica", "section", None, "tensor")
    outs = (wide, P("section", "replica", "tensor"), P("section", "tensor"))
    return jax.shard_map(
        gathered if few else reduced,
        mesh=mesh,
        in_specs=(wide, wide, P("section", "tensor", None), outs[1], P("replica", "section", "tensor"), outs[2]),
        out_specs=outs,
        check_vma=False,
    )
```

```python
import functools

import jax
import jax.numpy as jnp
from jax import lax
from jax.experimental import pallas as pl
from jax.experimental.pallas import tpu as pltpu
from jax.sharding import PartitionSpec as P

ROUNDS = 2
GATHER_MAX = 8
PAD = 16
CHUNKS = 4
STEP = 8
HIGHEST = lax.Precision.HIGHEST
F32, BF16 = jnp.float32, jnp.bfloat16
VMEM = pl.BlockSpec(memory_space=pltpu.VMEM)
HBM = pl.BlockSpec(memory_space=pltpu.MemorySpace.HBM)


def dot(a, b, ca, cb, precision=None):
    return lax.dot_general(a, b, (((ca,), (cb,)), ((), ())), precision=precision, preferred_element_type=F32)


def call(kernel, outs, *args, flops=0, in_specs=None, out_specs=None, scratch=(), limit=32, cost=None):
    size = sum(a.size * a.dtype.itemsize for a in (*args, *outs))
    return pl.pallas_call(
        kernel,
        out_shape=outs,
        in_specs=in_specs or [VMEM] * len(args),
        out_specs=out_specs or [VMEM] * len(outs),
        scratch_shapes=scratch,
        compiler_params=pltpu.CompilerParams(vmem_limit_bytes=limit * 1024 * 1024),
        cost_estimate=pl.CostEstimate(flops=flops, bytes_accessed=cost or size, transcendentals=0),
    )(*args)


def three_parts(x):
    hi = x.astype(BF16).astype(F32)
    mid = (x - hi).astype(BF16).astype(F32)
    lo = (x - hi - mid).astype(BF16).astype(F32)
    return hi, mid, lo


def tree(values):
    values = list(values)
    while len(values) > 1:
        values = [a + b for a, b in zip(values[::2], values[1::2])] + values[len(values) & ~1 :]
    return values[0]


def inverse_factor(gram):
    n = gram.shape[0]
    wide = max(128, 2 * n)
    eye = (lax.broadcasted_iota(jnp.int32, (n, n), 0) == lax.broadcasted_iota(jnp.int32, (n, n), 1)).astype(F32)
    row = lax.broadcasted_iota(jnp.int32, (n, wide), 0)
    both = jnp.concatenate([gram, eye, jnp.zeros((n, wide - 2 * n), F32)], axis=1)
    scale = jnp.zeros((n, wide), F32)
    for first in range(0, n, STEP):
        columns = [jnp.broadcast_to(both[:, k : k + 1], (n, wide)) for k in range(first, first + STEP)]
        for j in range(STEP):
            k = first + j
            inverse = 1.0 / jnp.broadcast_to(columns[j][k : k + 1, :], (n, wide))
            scale = jnp.where(row == k, inverse, scale)
            factor = jnp.where(row > k, columns[j] * inverse, 0.0)
            for i in range(j + 1, STEP):
                columns[i] = columns[i] - factor * columns[i][k : k + 1, :]
            both = both - factor * both[k : k + 1, :]
    return both[:, n : 2 * n] * jnp.sqrt(scale[:, :n])


def merge_kernel(grads, errors, q, vec, merged, p_part, grads_in, errors_in, q_in, vec_in, sems):
    rows, cols = grads.shape
    step = rows // CHUNKS
    small = [pltpu.make_async_copy(a, b, sems.at[2, i]) for i, (a, b) in enumerate([(q, q_in), (vec, vec_in)])]
    large = [
        [
            pltpu.make_async_copy(a.at[pl.ds(i * step, step)], b.at[pl.ds(i * step, step)], sems.at[j, i])
            for j, (a, b) in enumerate([(grads, grads_in), (errors, errors_in)])
        ]
        for i in range(CHUNKS)
    ]
    for copy in small + sum(large, []):
        copy.start()
    for copy in small:
        copy.wait()
    q_lo = q_in[...].astype(BF16)
    parts = three_parts(vec_in[...])
    merged[rows:, :] = jnp.concatenate([*parts, jnp.zeros((PAD - 3, cols), F32)], axis=0).astype(BF16)
    for i in range(CHUNKS):
        for copy in large[i]:
            copy.wait()
        here = slice(i * step, (i + 1) * step)
        total = (grads_in[here, :].astype(F32) + errors_in[here, :].astype(F32)).astype(BF16)
        merged[here, :] = total
        p_part[:, here] = dot(q_lo, total, 1, 1)


def add_kernel(*refs):
    refs[-1][...] = tree([r[...] for r in refs[:-1]])


def factor_kernel(n_p, replicas, last, owner, *refs):
    @pl.when(lax.axis_index("replica") == owner[0] + lax.axis_index("section") * (owner[-1] - owner[0]))
    def _():
        factor_step(refs[:n_p], refs[n_p:-1], refs[-1], replicas, last)


def factor_step(p_parts, merged, out, replicas, last):
    rows, cols = merged[0].shape[0] - PAD, merged[0].shape[1]
    p_sum = tree([p[...] for p in p_parts]) * (1.0 / replicas)
    inverse = inverse_factor(dot(p_sum, p_sum, 1, 1, HIGHEST))
    p_lo = dot(inverse, p_sum, 1, 0, HIGHEST).astype(BF16)
    q_sum = tree([dot(p_lo, m[:rows, :], 1, 0) for m in merged])
    q_lo = (q_sum * (1.0 / replicas)).astype(BF16)
    if not last:
        out[...] = tree([dot(q_lo, m[:rows, :], 1, 1) for m in merged])
        return
    out[:, :rows] = p_lo
    out[:, rows : rows + cols] = q_lo
    vec = tree([jnp.sum(m[rows:, :].astype(F32), axis=0, keepdims=True) for m in merged]) * (1.0 / replicas)
    parts = three_parts(vec)
    out[:, rows + cols :] = jnp.concatenate([*parts, jnp.zeros((out.shape[0] - 3, cols), F32)], axis=0).astype(BF16)


def final_kernel(sources, merged, momentum, vec_momentum, *refs):
    packs = refs[:-9]
    new_errors, new_momentum, new_vec, pack, p_rows, errors_out, momentum_out, vec_out, sems = refs[-9:]
    rows, cols = new_errors.shape
    own_rows = momentum.shape[0]
    z, s = lax.axis_index("replica"), lax.axis_index("section")
    came = sum(
        jnp.where((z == row[j]) & (s == i), j + 1, 0) for i, row in enumerate(sources) for j in range(len(row))
    )
    for i, candidate in enumerate(packs):

        @pl.when(came == i)
        def _(candidate=candidate):
            pack[...] = candidate[...]

    p_rows[...] = pack[:, :rows].T
    q_lo = pack[:, rows : rows + cols]
    copies = []
    step = rows // CHUNKS
    for i in range(CHUNKS):
        here = pl.ds(i * step, step)
        approx = dot(p_rows[here, :], q_lo, 1, 0)
        errors_out[here, :] = (merged[here, :].astype(F32) - approx).astype(BF16)
        copies.append(pltpu.make_async_copy(errors_out.at[here], new_errors.at[here], sems.at[i]))
        copies[-1].start()
    first = pl.multiple_of(z * own_rows, own_rows)
    mine = dot(p_rows[pl.ds(first, own_rows), :], q_lo, 1, 0)
    momentum_out[...] = 0.9 * momentum[...] + mine
    copies.append(pltpu.make_async_copy(momentum_out, new_momentum, sems.at[CHUNKS]))
    copies[-1].start()
    vec = jnp.sum(pack[:, rows + cols :].astype(F32), axis=0, keepdims=True)
    vec_out[...] = 0.9 * vec_momentum[...] + vec
    copies.append(pltpu.make_async_copy(vec_out, new_vec, sems.at[CHUNKS + 1]))
    copies[-1].start()
    for copy in copies:
        copy.wait()


def completed(needed, places):
    needed = list(needed)
    sources = [p for p in places if p not in [a for a, _ in needed]]
    targets = [p for p in places if p not in [b for _, b in needed]]
    far = {(a, b): (a == b, 2 * abs(a[0] - b[0]) + (a[1] != b[1]), a, b) for a in sources for b in targets}
    for a, b in sorted(far, key=far.get):
        if a in sources and b in targets:
            sources.remove(a)
            targets.remove(b)
            needed.append((a, b))
    return needed


def gathered(grads, errors, q_start, momentum, vec_grads, vec_momentum):
    replicas, tensors, sections = (lax.axis_size(a) for a in ("replica", "tensor", "section"))
    rows, cols = grads.shape[2:]
    rank = q_start.shape[2]
    middle = (replicas - 1) // 2
    distance = lambda z, o: (-(abs(2 * z - replicas + 1) <= 1), -abs(z - o))
    owner = [middle + s % min(2, replicas) for s in range(sections)]
    sources = [sorted((z for z in range(replicas) if z != o), key=lambda z, o=o: distance(z, o)) for o in owner]
    places = [(z, s) for z in range(replicas) for s in range(sections)]
    inward = [
        completed([((sources[s][j], s), (owner[s], s)) for s in range(sections)], places) for j in range(replicas - 1)
    ]
    outward = [[(b, a) for a, b in pairs] for pairs in inward]
    number = lambda place: place[0] * sections + place[1]

    def along(x, perms):
        return [lax.ppermute(x, ("replica", "section"), [(number(a), number(b)) for a, b in p]) for p in perms]

    def across(x, steps):
        parts = [x]
        for k in steps:
            busy = [z for z in range(replicas) if z in owner]
            idle = [p for p in places if p[0] not in busy]
            pairs = [((z, i, s), (z, i ^ k, s)) for z in busy for s in range(sections) for i in range(tensors)]
            pairs += [((a[0], i, a[1]), (b[0], i, b[1])) for a, b in completed([], idle) for i in range(tensors)]
            order = [((a[0] * tensors + a[1]) * sections + a[2], (b[0] * tensors + b[1]) * sections + b[2]) for a, b in pairs]
            parts.append(lax.ppermute(x, ("replica", "tensor", "section"), order))
        return parts

    p_shape = jax.ShapeDtypeStruct((rank, rows), F32)
    work = 2 * rows * cols * rank
    block = (rows, cols)
    merged_shape = jax.ShapeDtypeStruct((rows + PAD, cols), BF16)
    merged, p_part = call(
        merge_kernel,
        [merged_shape, p_shape],
        *(pltpu.with_memory_space_constraint(x, pltpu.HBM) for x in (grads[0, 0], errors[0, 0], q_start[0].T, vec_grads[0])),
        flops=work,
        in_specs=[HBM] * 4,
        scratch=[
            pltpu.VMEM(block, BF16),
            pltpu.VMEM(block, BF16),
            pltpu.VMEM((rank, cols), F32),
            pltpu.VMEM((1, cols), F32),
            pltpu.SemaphoreType.DMA((3, CHUNKS)),
        ],
    )
    p_in = along(p_part, inward)
    m_near = along(merged, inward[:1] + inward[2:])
    p_part = call(add_kernel, [p_shape], p_part, *p_in)[0]
    held = lax.optimization_barrier((merged, p_part))[0]
    m_in = along(held, inward[1:2]) + m_near
    for round_no in range(ROUNDS):
        last = round_no == ROUNDS - 1
        shape = jax.ShapeDtypeStruct((rank, rows + 2 * cols), BF16) if last else p_shape
        if round_no:
            parts = across(p_part, range(1, tensors))
        else:
            k = 1
            while 2 * k < tensors:
                p_part = tree(across(p_part, [k]))
                k *= 2
            parts = across(p_part, [k] if k < tensors else [])
        p_part = call(
            functools.partial(factor_kernel, len(parts), replicas, last, owner),
            [shape],
            *parts,
            merged,
            *m_in,
            flops=2 * replicas * work,
        )[0]
    received = along(p_part, outward)
    new_errors, new_momentum, new_vec = call(
        functools.partial(final_kernel, sources),
        [
            jax.ShapeDtypeStruct(block, BF16),
            jax.ShapeDtypeStruct(momentum.shape[1:], F32),
            jax.ShapeDtypeStruct((1, cols), F32),
        ],
        merged,
        momentum[0],
        vec_momentum,
        p_part,
        *received,
        flops=2 * work,
        out_specs=[HBM] * 3,
        scratch=[
            pltpu.VMEM(p_part.shape, BF16),
            pltpu.VMEM((rows, rank), BF16),
            pltpu.VMEM(block, BF16),
            pltpu.VMEM(momentum.shape[1:], F32),
            pltpu.VMEM((1, cols), F32),
            pltpu.SemaphoreType.DMA((CHUNKS + 2,)),
        ],
    )
    return new_errors[None, None], new_momentum[None], new_vec


def reduced(grads, errors, q_start, momentum, vec_grads, vec_momentum):
    replicas = lax.axis_size("replica")
    merged = (grads[0].astype(F32) + errors[0].astype(F32)).astype(BF16)
    q_lo = q_start.astype(BF16)
    vec_sum = lax.psum(vec_grads[0], "replica")
    p_lo = None
    for _ in range(ROUNDS):
        p_part = jnp.einsum("bdc,bcr->brd", merged, q_lo, preferred_element_type=F32)
        p_sum = lax.psum(p_part, ("replica", "tensor")) / replicas
        gram = jnp.einsum("brd,bsd->brs", p_sum, p_sum, precision=HIGHEST)
        inverse = jnp.stack([inverse_factor(g) for g in gram])
        p_lo = jnp.einsum("brs,bsd->brd", inverse, p_sum, precision=HIGHEST).astype(BF16)
        q_part = jnp.einsum("bdc,brd->bcr", merged, p_lo, preferred_element_type=F32)
        q_lo = (lax.psum(q_part, "replica") / replicas).astype(BF16)
    approx = jnp.einsum("brd,bcr->bdc", p_lo, q_lo, preferred_element_type=F32)
    new_errors = (merged.astype(F32) - approx).astype(BF16)[None]
    own_rows = momentum.shape[1]
    mine = lax.dynamic_slice_in_dim(approx, lax.axis_index("replica") * own_rows, own_rows, 1)
    return new_errors, 0.9 * momentum + mine, 0.9 * vec_momentum + vec_sum / replicas


def solution(mesh):
    few = mesh.shape["replica"] <= GATHER_MAX
    wide = P("replica", "section", None, "tensor")
    outs = (wide, P("section", "replica", "tensor"), P("section", "tensor"))
    return jax.shard_map(
        gathered if few else reduced,
        mesh=mesh,
        in_specs=(wide, wide, P("section", "tensor", None), outs[1], P("replica", "section", "tensor"), outs[2]),
        out_specs=outs,
        check_vma=False,
    )
```

```python
import functools

import jax
import jax.numpy as jnp
from jax import lax
from jax.experimental import pallas as pl
from jax.experimental.pallas import tpu as pltpu
from jax.sharding import PartitionSpec as P

ROUNDS = 2
GATHER_MAX = 8
PAD = 16
CHUNKS = 4
STEP = 16
HIGHEST = lax.Precision.HIGHEST
F32, BF16 = jnp.float32, jnp.bfloat16
VMEM = pl.BlockSpec(memory_space=pltpu.VMEM)
HBM = pl.BlockSpec(memory_space=pltpu.MemorySpace.HBM)


def dot(a, b, ca, cb, precision=None):
    return lax.dot_general(a, b, (((ca,), (cb,)), ((), ())), precision=precision, preferred_element_type=F32)


def call(kernel, outs, *args, flops=0, in_specs=None, out_specs=None, scratch=(), limit=32, cost=None):
    size = sum(a.size * a.dtype.itemsize for a in (*args, *outs))
    return pl.pallas_call(
        kernel,
        out_shape=outs,
        in_specs=in_specs or [VMEM] * len(args),
        out_specs=out_specs or [VMEM] * len(outs),
        scratch_shapes=scratch,
        compiler_params=pltpu.CompilerParams(vmem_limit_bytes=limit * 1024 * 1024),
        cost_estimate=pl.CostEstimate(flops=flops, bytes_accessed=cost or size, transcendentals=0),
    )(*args)


def three_parts(x):
    hi = x.astype(BF16).astype(F32)
    mid = (x - hi).astype(BF16).astype(F32)
    lo = (x - hi - mid).astype(BF16).astype(F32)
    return hi, mid, lo


def tree(values):
    values = list(values)
    while len(values) > 1:
        values = [a + b for a, b in zip(values[::2], values[1::2])] + values[len(values) & ~1 :]
    return values[0]


def inverse_factor(gram):
    n = gram.shape[0]
    wide = max(128, 2 * n)
    eye = (lax.broadcasted_iota(jnp.int32, (n, n), 0) == lax.broadcasted_iota(jnp.int32, (n, n), 1)).astype(F32)
    row = lax.broadcasted_iota(jnp.int32, (n, wide), 0)
    both = jnp.concatenate([gram, eye, jnp.zeros((n, wide - 2 * n), F32)], axis=1)
    scale = jnp.zeros((n, wide), F32)
    for first in range(0, n, STEP):
        columns = [jnp.broadcast_to(both[:, k : k + 1], (n, wide)) for k in range(first, first + STEP)]
        for j in range(STEP):
            k = first + j
            inverse = 1.0 / jnp.broadcast_to(columns[j][k : k + 1, :], (n, wide))
            scale = jnp.where(row == k, inverse, scale)
            factor = jnp.where(row > k, columns[j] * inverse, 0.0)
            for i in range(j + 1, STEP):
                columns[i] = columns[i] - factor * columns[i][k : k + 1, :]
            both = both - factor * both[k : k + 1, :]
    return both[:, n : 2 * n] * jnp.sqrt(scale[:, :n])


def merge_kernel(grads, errors, q, vec, merged, p_part, grads_in, errors_in, q_in, vec_in, sems):
    rows, cols = grads.shape
    step = rows // CHUNKS
    small = [pltpu.make_async_copy(a, b, sems.at[2, i]) for i, (a, b) in enumerate([(q, q_in), (vec, vec_in)])]
    large = [
        [
            pltpu.make_async_copy(a.at[pl.ds(i * step, step)], b.at[pl.ds(i * step, step)], sems.at[j, i])
            for j, (a, b) in enumerate([(grads, grads_in), (errors, errors_in)])
        ]
        for i in range(CHUNKS)
    ]
    for copy in small + sum(large, []):
        copy.start()
    for copy in small:
        copy.wait()
    q_lo = q_in[...].astype(BF16)
    parts = three_parts(vec_in[...])
    merged[rows:, :] = jnp.concatenate([*parts, jnp.zeros((PAD - 3, cols), F32)], axis=0).astype(BF16)
    for i in range(CHUNKS):
        for copy in large[i]:
            copy.wait()
        here = slice(i * step, (i + 1) * step)
        total = (grads_in[here, :].astype(F32) + errors_in[here, :].astype(F32)).astype(BF16)
        merged[here, :] = total
        p_part[:, here] = dot(q_lo, total, 1, 1)


def add_kernel(*refs):
    refs[-1][...] = tree([r[...] for r in refs[:-1]])


def own_block(owner):
    return lax.axis_index("replica") == owner[0] + lax.axis_index("section") * (owner[-1] - owner[0])


def factor_kernel(replicas, owner, *refs):
    @pl.when(own_block(owner))
    def _():
        p_sum = tree([p[...] for p in refs[:-1]]) * (1.0 / replicas)
        inverse = inverse_factor(dot(p_sum, p_sum, 1, 1, HIGHEST))
        refs[-1][...] = dot(inverse, p_sum, 1, 0, HIGHEST).astype(BF16)


def turn_kernel(replicas, last, owner, p_lo, *refs):
    merged, out = refs[:-1], refs[-1]
    rows, cols = merged[0].shape[0] - PAD, merged[0].shape[1]

    @pl.when(own_block(owner))
    def _():
        q_sum = tree([dot(p_lo[...], m[:rows, :], 1, 0) for m in merged])
        q_lo = (q_sum * (1.0 / replicas)).astype(BF16)
        if not last:
            out[...] = tree([dot(q_lo, m[:rows, :], 1, 1) for m in merged])
            return
        out[:, :rows] = p_lo[...]
        out[:, rows : rows + cols] = q_lo
        vec = tree([jnp.sum(m[rows:, :].astype(F32), axis=0, keepdims=True) for m in merged]) * (1.0 / replicas)
        fill = jnp.zeros((out.shape[0] - 3, cols), F32)
        out[:, rows + cols :] = jnp.concatenate([*three_parts(vec), fill], axis=0).astype(BF16)


def final_kernel(sources, merged, momentum, vec_momentum, *refs):
    packs = refs[:-9]
    new_errors, new_momentum, new_vec, pack, p_rows, errors_out, momentum_out, vec_out, sems = refs[-9:]
    rows, cols = new_errors.shape
    own_rows = momentum.shape[0]
    z, s = lax.axis_index("replica"), lax.axis_index("section")
    came = sum(
        jnp.where((z == row[j]) & (s == i), j + 1, 0) for i, row in enumerate(sources) for j in range(len(row))
    )
    for i, candidate in enumerate(packs):

        @pl.when(came == i)
        def _(candidate=candidate):
            pack[...] = candidate[...]

    p_rows[...] = pack[:, :rows].T
    q_lo = pack[:, rows : rows + cols]
    copies = []
    step = rows // CHUNKS
    for i in range(CHUNKS):
        here = pl.ds(i * step, step)
        approx = dot(p_rows[here, :], q_lo, 1, 0)
        errors_out[here, :] = (merged[here, :].astype(F32) - approx).astype(BF16)
        copies.append(pltpu.make_async_copy(errors_out.at[here], new_errors.at[here], sems.at[i]))
        copies[-1].start()
    first = pl.multiple_of(z * own_rows, own_rows)
    mine = dot(p_rows[pl.ds(first, own_rows), :], q_lo, 1, 0)
    momentum_out[...] = 0.9 * momentum[...] + mine
    copies.append(pltpu.make_async_copy(momentum_out, new_momentum, sems.at[CHUNKS]))
    copies[-1].start()
    vec = jnp.sum(pack[:, rows + cols :].astype(F32), axis=0, keepdims=True)
    vec_out[...] = 0.9 * vec_momentum[...] + vec
    copies.append(pltpu.make_async_copy(vec_out, new_vec, sems.at[CHUNKS + 1]))
    copies[-1].start()
    for copy in copies:
        copy.wait()


def completed(needed, places):
    needed = list(needed)
    sources = [p for p in places if p not in [a for a, _ in needed]]
    targets = [p for p in places if p not in [b for _, b in needed]]
    far = {(a, b): (a == b, 2 * abs(a[0] - b[0]) + (a[1] != b[1]), a, b) for a in sources for b in targets}
    for a, b in sorted(far, key=far.get):
        if a in sources and b in targets:
            sources.remove(a)
            targets.remove(b)
            needed.append((a, b))
    return needed


def gathered(grads, errors, q_start, momentum, vec_grads, vec_momentum):
    replicas, tensors, sections = (lax.axis_size(a) for a in ("replica", "tensor", "section"))
    rows, cols = grads.shape[2:]
    rank = q_start.shape[2]
    middle = (replicas - 1) // 2
    distance = lambda z, o: (-(abs(2 * z - replicas + 1) <= 1), -abs(z - o))
    owner = [middle + s % min(2, replicas) for s in range(sections)]
    sources = [sorted((z for z in range(replicas) if z != o), key=lambda z, o=o: distance(z, o)) for o in owner]
    places = [(z, s) for z in range(replicas) for s in range(sections)]
    inward = [
        completed([((sources[s][j], s), (owner[s], s)) for s in range(sections)], places) for j in range(replicas - 1)
    ]
    outward = [[(b, a) for a, b in pairs] for pairs in inward]
    number = lambda place: place[0] * sections + place[1]

    def along(x, perms):
        return [lax.ppermute(x, ("replica", "section"), [(number(a), number(b)) for a, b in p]) for p in perms]

    def across(x, steps, busy):
        parts = [x]
        for k in steps:
            idle = [p for p in places if p not in busy]
            pairs = [((z, i, s), (z, i ^ k, s)) for z, s in busy for i in range(tensors)]
            pairs += [((a[0], i, a[1]), (b[0], i, b[1])) for a, b in completed([], idle) for i in range(tensors)]
            order = [((a[0] * tensors + a[1]) * sections + a[2], (b[0] * tensors + b[1]) * sections + b[2]) for a, b in pairs]
            parts.append(lax.ppermute(x, ("replica", "tensor", "section"), order))
        return parts

    p_shape = jax.ShapeDtypeStruct((rank, rows), F32)
    work = 2 * rows * cols * rank
    block = (rows, cols)
    merged_shape = jax.ShapeDtypeStruct((rows + PAD, cols), BF16)
    merged, p_part = call(
        merge_kernel,
        [merged_shape, p_shape],
        *(pltpu.with_memory_space_constraint(x, pltpu.HBM) for x in (grads[0, 0], errors[0, 0], q_start[0].T, vec_grads[0])),
        flops=work,
        in_specs=[HBM] * 4,
        scratch=[
            pltpu.VMEM(block, BF16),
            pltpu.VMEM(block, BF16),
            pltpu.VMEM((rank, cols), F32),
            pltpu.VMEM((1, cols), F32),
            pltpu.SemaphoreType.DMA((3, CHUNKS)),
        ],
    )
    planes = [p for p in places if p[0] in owner]
    p_in = along(p_part, inward)
    m_near = along(merged, inward[:1] + inward[2:])
    p_part = call(add_kernel, [p_shape], p_part, *p_in)[0]
    held = lax.optimization_barrier((merged, p_part))[0]
    m_in = along(held, inward[1:2]) + m_near
    for round_no in range(ROUNDS):
        last = round_no == ROUNDS - 1
        shape = jax.ShapeDtypeStruct((rank, rows + 2 * cols), BF16) if last else p_shape
        if round_no:
            parts = across(p_part, range(1, tensors), [(owner[s], s) for s in range(sections)])
        else:
            k = 1
            while 2 * k < tensors:
                p_part = tree(across(p_part, [k], planes))
                k *= 2
            parts = across(p_part, [k] if k < tensors else [], planes)
        p_lo = call(
            functools.partial(factor_kernel, replicas, owner), [jax.ShapeDtypeStruct((rank, rows), BF16)], *parts
        )[0]
        p_part = call(
            functools.partial(turn_kernel, replicas, last, owner),
            [shape],
            p_lo,
            merged,
            *m_in,
            flops=2 * replicas * work,
        )[0]
    received = along(p_part, outward)
    new_errors, new_momentum, new_vec = call(
        functools.partial(final_kernel, sources),
        [
            jax.ShapeDtypeStruct(block, BF16),
            jax.ShapeDtypeStruct(momentum.shape[1:], F32),
            jax.ShapeDtypeStruct((1, cols), F32),
        ],
        merged,
        momentum[0],
        vec_momentum,
        p_part,
        *received,
        flops=2 * work,
        out_specs=[HBM] * 3,
        scratch=[
            pltpu.VMEM(p_part.shape, BF16),
            pltpu.VMEM((rows, rank), BF16),
            pltpu.VMEM(block, BF16),
            pltpu.VMEM(momentum.shape[1:], F32),
            pltpu.VMEM((1, cols), F32),
            pltpu.SemaphoreType.DMA((CHUNKS + 2,)),
        ],
    )
    return new_errors[None, None], new_momentum[None], new_vec


def reduced(grads, errors, q_start, momentum, vec_grads, vec_momentum):
    replicas = lax.axis_size("replica")
    merged = (grads[0].astype(F32) + errors[0].astype(F32)).astype(BF16)
    q_lo = q_start.astype(BF16)
    vec_sum = lax.psum(vec_grads[0], "replica")
    p_lo = None
    for _ in range(ROUNDS):
        p_part = jnp.einsum("bdc,bcr->brd", merged, q_lo, preferred_element_type=F32)
        p_sum = lax.psum(p_part, ("replica", "tensor")) / replicas
        gram = jnp.einsum("brd,bsd->brs", p_sum, p_sum, precision=HIGHEST)
        inverse = jnp.stack([inverse_factor(g) for g in gram])
        p_lo = jnp.einsum("brs,bsd->brd", inverse, p_sum, precision=HIGHEST).astype(BF16)
        q_part = jnp.einsum("bdc,brd->bcr", merged, p_lo, preferred_element_type=F32)
        q_lo = (lax.psum(q_part, "replica") / replicas).astype(BF16)
    approx = jnp.einsum("brd,bcr->bdc", p_lo, q_lo, preferred_element_type=F32)
    new_errors = (merged.astype(F32) - approx).astype(BF16)[None]
    own_rows = momentum.shape[1]
    mine = lax.dynamic_slice_in_dim(approx, lax.axis_index("replica") * own_rows, own_rows, 1)
    return new_errors, 0.9 * momentum + mine, 0.9 * vec_momentum + vec_sum / replicas


def solution(mesh):
    few = mesh.shape["replica"] <= GATHER_MAX
    wide = P("replica", "section", None, "tensor")
    outs = (wide, P("section", "replica", "tensor"), P("section", "tensor"))
    return jax.shard_map(
        gathered if few else reduced,
        mesh=mesh,
        in_specs=(wide, wide, P("section", "tensor", None), outs[1], P("replica", "section", "tensor"), outs[2]),
        out_specs=outs,
        check_vma=False,
    )
```

```python
import functools

import jax
import jax.numpy as jnp
from jax import lax
from jax.experimental import pallas as pl
from jax.experimental.pallas import tpu as pltpu
from jax.sharding import PartitionSpec as P

ROUNDS = 2
LANES = 128
PAD = 16
CHUNKS_IN, CHUNKS_OUT = 2, 4
STEP = 16
HIGHEST = lax.Precision.HIGHEST
F32, BF16 = jnp.float32, jnp.bfloat16
VMEM = pl.BlockSpec(memory_space=pltpu.VMEM)
HBM = pl.BlockSpec(memory_space=pltpu.MemorySpace.HBM)


def dot(a, b, ca, cb, precision=None):
    return lax.dot_general(a, b, (((ca,), (cb,)), ((), ())), precision=precision, preferred_element_type=F32)


def call(kernel, outs, *args, flops=0, in_specs=None, out_specs=None, scratch=(), limit=32, cost=None):
    size = sum(a.size * a.dtype.itemsize for a in (*args, *outs))
    return pl.pallas_call(
        kernel,
        out_shape=outs,
        in_specs=in_specs or [VMEM] * len(args),
        out_specs=out_specs or [VMEM] * len(outs),
        scratch_shapes=scratch,
        compiler_params=pltpu.CompilerParams(vmem_limit_bytes=limit * 1024 * 1024),
        cost_estimate=pl.CostEstimate(flops=flops, bytes_accessed=cost or size, transcendentals=0),
    )(*args)


def three_parts(x):
    hi = x.astype(BF16).astype(F32)
    mid = (x - hi).astype(BF16).astype(F32)
    lo = (x - hi - mid).astype(BF16).astype(F32)
    return hi, mid, lo


def tree(values):
    values = list(values)
    while len(values) > 1:
        values = [a + b for a, b in zip(values[::2], values[1::2])] + values[len(values) & ~1 :]
    return values[0]


def inverse_factor(gram):
    n = gram.shape[0]
    wide = max(128, 2 * n)
    eye = (lax.broadcasted_iota(jnp.int32, (n, n), 0) == lax.broadcasted_iota(jnp.int32, (n, n), 1)).astype(F32)
    row = lax.broadcasted_iota(jnp.int32, (n, wide), 0)
    both = jnp.concatenate([gram, eye, jnp.zeros((n, wide - 2 * n), F32)], axis=1)
    scale = jnp.zeros((n, wide), F32)
    for first in range(0, n, STEP):
        columns = [jnp.broadcast_to(both[:, k : k + 1], (n, wide)) for k in range(first, first + STEP)]
        for j in range(STEP):
            k = first + j
            inverse = 1.0 / jnp.broadcast_to(columns[j][k : k + 1, :], (n, wide))
            scale = jnp.where(row == k, inverse, scale)
            factor = jnp.where(row > k, columns[j] * inverse, 0.0)
            for i in range(j + 1, STEP):
                columns[i] = columns[i] - factor * columns[i][k : k + 1, :]
            both = both - factor * both[k : k + 1, :]
    return both[:, n : 2 * n] * jnp.sqrt(scale[:, :n])


def merge_kernel(grads, errors, q, vec, merged, p_part, grads_in, errors_in, q_in, vec_in, sems):
    rows, cols = grads.shape
    step = rows // CHUNKS_IN
    small = [pltpu.make_async_copy(a, b, sems.at[2, i]) for i, (a, b) in enumerate([(q, q_in), (vec, vec_in)])]
    large = [
        [
            pltpu.make_async_copy(a.at[pl.ds(i * step, step)], b.at[pl.ds(i * step, step)], sems.at[j, i])
            for j, (a, b) in enumerate([(grads, grads_in), (errors, errors_in)])
        ]
        for i in range(CHUNKS_IN)
    ]
    for copy in small + sum(large, []):
        copy.start()
    for copy in small:
        copy.wait()
    q_lo = q_in[...].astype(BF16)
    parts = three_parts(vec_in[...])
    merged[rows:, :] = jnp.concatenate([*parts, jnp.zeros((PAD - 3, cols), F32)], axis=0).astype(BF16)
    for i in range(CHUNKS_IN):
        for copy in large[i]:
            copy.wait()
        here = slice(i * step, (i + 1) * step)
        total = (grads_in[here, :].astype(F32) + errors_in[here, :].astype(F32)).astype(BF16)
        merged[here, :] = total
        p_part[:, here] = dot(q_lo, total, 1, 1)


def add_kernel(*refs):
    refs[-1][...] = tree([r[...] for r in refs[:-1]])


def own_block(owner):
    return lax.axis_index("replica") == owner[0] + lax.axis_index("section") * (owner[-1] - owner[0])


def factor_kernel(replicas, owner, *refs):
    @pl.when(own_block(owner))
    def _():
        p_sum = tree([p[...] for p in refs[:-1]]) * (1.0 / replicas)
        inverse = inverse_factor(dot(p_sum, p_sum, 1, 1, HIGHEST))
        refs[-1][...] = dot(inverse, p_sum, 1, 0, HIGHEST).astype(BF16)


def product(left, mean, here, axis):
    high, low = mean
    return dot(left, high[here, :], 1, axis) + dot(left, low[here, :], 1, axis)


def turn_kernel(replicas, owner, p_lo, *refs):
    *merged, high, low, vec_mean, out = refs
    rows = high.shape[0]

    @pl.when(own_block(owner))
    def _():
        total = tree([m[:rows, :].astype(F32) for m in merged]) * (1.0 / replicas)
        top = total.astype(BF16)
        high[...] = top
        low[...] = (total - top.astype(F32)).astype(BF16)
        vec_mean[...] = tree([jnp.sum(m[rows:, :].astype(F32), axis=0, keepdims=True) for m in merged]) * (1.0 / replicas)
        everything = slice(0, rows)
        q_lo = product(p_lo[...], (high, low), everything, 0).astype(BF16)
        out[...] = product(q_lo, (high, low), everything, 1)


def last_kernel(owner, p_lo, high, low, vec_mean, out):
    rows, cols = high.shape

    @pl.when(own_block(owner))
    def _():
        q_lo = product(p_lo[...], (high, low), slice(0, rows), 0).astype(BF16)
        vec = vec_mean[...]
        parts = [part[:, i : i + LANES] for part in three_parts(vec) for i in range(0, cols, LANES)]
        fill = jnp.zeros((out.shape[0] - len(parts), LANES), F32)
        out[:, :rows] = p_lo[...]
        out[:, rows : rows + cols] = q_lo
        out[:, rows + cols :] = jnp.concatenate([*parts, fill], axis=0).astype(BF16)


def final_kernel(sources, merged, momentum, vec_momentum, *refs):
    packs = refs[:-9]
    new_errors, new_momentum, new_vec, rest, p_rows, errors_out, momentum_out, vec_out, sems = refs[-9:]
    rows, cols = new_errors.shape
    own_rows = momentum.shape[0]
    z, s = lax.axis_index("replica"), lax.axis_index("section")
    came = sum(
        jnp.where((z == row[j]) & (s == i), j + 1, 0) for i, row in enumerate(sources) for j in range(len(row))
    )
    for i, pack in enumerate(packs):

        @pl.when(came == i)
        def _(pack=pack):
            p_rows[...] = pack[:, :rows].T
            rest[...] = pack[:, rows:]

    q_lo = rest[:, :cols]
    copies = []
    step = rows // CHUNKS_OUT
    for i in range(CHUNKS_OUT):
        here = pl.ds(i * step, step)
        approx = dot(p_rows[here, :], q_lo, 1, 0)
        errors_out[here, :] = (merged[here, :].astype(F32) - approx).astype(BF16)
        copies.append(pltpu.make_async_copy(errors_out.at[here], new_errors.at[here], sems.at[i]))
        copies[-1].start()
    start = pl.multiple_of(z * own_rows, own_rows)
    mine = dot(p_rows[pl.ds(start, own_rows), :], q_lo, 1, 0)
    momentum_out[...] = 0.9 * momentum[...] + mine
    copies.append(pltpu.make_async_copy(momentum_out, new_momentum, sems.at[CHUNKS_OUT]))
    copies[-1].start()
    parts = rest[:, cols:].astype(F32)
    pieces = cols // LANES
    for i in range(pieces):
        vec = parts[i : i + 1] + parts[pieces + i : pieces + i + 1] + parts[2 * pieces + i : 2 * pieces + i + 1]
        here = slice(i * LANES, (i + 1) * LANES)
        vec_out[:, here] = 0.9 * vec_momentum[:, here] + vec
    copies.append(pltpu.make_async_copy(vec_out, new_vec, sems.at[CHUNKS_OUT + 1]))
    copies[-1].start()
    for copy in copies:
        copy.wait()


def completed(needed, places):
    needed = list(needed)
    sources = [p for p in places if p not in [a for a, _ in needed]]
    targets = [p for p in places if p not in [b for _, b in needed]]
    far = {(a, b): (a == b, 2 * abs(a[0] - b[0]) + (a[1] != b[1]), a, b) for a in sources for b in targets}
    for a, b in sorted(far, key=far.get):
        if a in sources and b in targets:
            sources.remove(a)
            targets.remove(b)
            needed.append((a, b))
    return needed


def gathered(grads, errors, q_start, momentum, vec_grads, vec_momentum):
    replicas, tensors, sections = (lax.axis_size(a) for a in ("replica", "tensor", "section"))
    rows, cols = grads.shape[2:]
    rank = q_start.shape[2]
    middle = (replicas - 1) // 2
    distance = lambda z, o: (-(abs(2 * z - replicas + 1) <= 1), -abs(z - o))
    owner = [middle + s % min(2, replicas) for s in range(sections)]
    sources = [sorted((z for z in range(replicas) if z != o), key=lambda z, o=o: distance(z, o)) for o in owner]
    places = [(z, s) for z in range(replicas) for s in range(sections)]
    inward = [
        completed([((sources[s][j], s), (owner[s], s)) for s in range(sections)], places) for j in range(replicas - 1)
    ]
    outward = [[(b, a) for a, b in pairs] for pairs in inward]
    number = lambda place: place[0] * sections + place[1]

    def along(x, perms):
        return [lax.ppermute(x, ("replica", "section"), [(number(a), number(b)) for a, b in p]) for p in perms]

    def across(x, steps, busy):
        parts = [x]
        for k in steps:
            idle = [p for p in places if p not in busy]
            pairs = [((z, i, s), (z, i ^ k, s)) for z, s in busy for i in range(tensors)]
            pairs += [((a[0], i, a[1]), (b[0], i, b[1])) for a, b in completed([], idle) for i in range(tensors)]
            order = [((a[0] * tensors + a[1]) * sections + a[2], (b[0] * tensors + b[1]) * sections + b[2]) for a, b in pairs]
            parts.append(lax.ppermute(x, ("replica", "tensor", "section"), order))
        return parts

    p_shape = jax.ShapeDtypeStruct((rank, rows), F32)
    work = 2 * rows * cols * rank
    block = (rows, cols)
    merged_shape = jax.ShapeDtypeStruct((rows + PAD, cols), BF16)
    merged, p_part = call(
        merge_kernel,
        [merged_shape, p_shape],
        *(pltpu.with_memory_space_constraint(x, pltpu.HBM) for x in (grads[0, 0], errors[0, 0], q_start[0].T, vec_grads[0])),
        flops=work,
        in_specs=[HBM] * 4,
        scratch=[
            pltpu.VMEM(block, BF16),
            pltpu.VMEM(block, BF16),
            pltpu.VMEM((rank, cols), F32),
            pltpu.VMEM((1, cols), F32),
            pltpu.SemaphoreType.DMA((3, CHUNKS_IN)),
        ],
    )
    planes = [p for p in places if p[0] in owner]
    p_in = along(p_part, inward)
    m_near = along(merged, inward[:1] + inward[2:])
    p_part = call(add_kernel, [p_shape], p_part, *p_in)[0]
    held = lax.optimization_barrier((merged, p_part))[0]
    m_in = along(held, inward[1:2]) + m_near
    k = 1
    while 2 * k < tensors:
        p_part = tree(across(p_part, [k], planes))
        k *= 2
    parts = across(p_part, [k] if k < tensors else [], planes)
    lo_shape = jax.ShapeDtypeStruct((rank, rows), BF16)
    for _ in range(ROUNDS - 1):
        p_lo = call(functools.partial(factor_kernel, replicas, owner), [lo_shape], *parts)[0]
        *mean, p_part = call(
            functools.partial(turn_kernel, replicas, owner),
            [jax.ShapeDtypeStruct(block, BF16)] * 2 + [jax.ShapeDtypeStruct((1, cols), F32), p_shape],
            p_lo,
            merged,
            *m_in,
            flops=4 * work,
        )
        parts = across(p_part, range(1, tensors), [(owner[s], s) for s in range(sections)])
    p_lo = call(functools.partial(factor_kernel, replicas, owner), [lo_shape], *parts)[0]
    whole = call(
        functools.partial(last_kernel, owner),
        [jax.ShapeDtypeStruct((rank, rows + cols + LANES), BF16)],
        p_lo,
        *mean,
        flops=2 * work,
    )[0]
    received = along(whole, outward)
    new_errors, new_momentum, new_vec = call(
        functools.partial(final_kernel, sources),
        [
            jax.ShapeDtypeStruct(block, BF16),
            jax.ShapeDtypeStruct(momentum.shape[1:], F32),
            jax.ShapeDtypeStruct((1, cols), F32),
        ],
        merged,
        momentum[0],
        vec_momentum,
        whole,
        *received,
        flops=2 * work,
        out_specs=[HBM] * 3,
        scratch=[
            pltpu.VMEM((rank, cols + LANES), BF16),
            pltpu.VMEM((rows, rank), BF16),
            pltpu.VMEM(block, BF16),
            pltpu.VMEM(momentum.shape[1:], F32),
            pltpu.VMEM((1, cols), F32),
            pltpu.SemaphoreType.DMA((CHUNKS_OUT + 2,)),
        ],
    )
    return new_errors[None, None], new_momentum[None], new_vec


def reduced(grads, errors, q_start, momentum, vec_grads, vec_momentum):
    replicas = lax.axis_size("replica")
    merged = (grads[0].astype(F32) + errors[0].astype(F32)).astype(BF16)
    q_lo = q_start.astype(BF16)
    vec_sum = lax.psum(vec_grads[0], "replica")
    p_lo = None
    for _ in range(ROUNDS):
        p_part = jnp.einsum("bdc,bcr->brd", merged, q_lo, preferred_element_type=F32)
        p_sum = lax.psum(p_part, ("replica", "tensor")) / replicas
        gram = jnp.einsum("brd,bsd->brs", p_sum, p_sum, precision=HIGHEST)
        inverse = jnp.stack([inverse_factor(g) for g in gram])
        p_lo = jnp.einsum("brs,bsd->brd", inverse, p_sum, precision=HIGHEST).astype(BF16)
        q_part = jnp.einsum("bdc,brd->bcr", merged, p_lo, preferred_element_type=F32)
        q_lo = (lax.psum(q_part, "replica") / replicas).astype(BF16)
    approx = jnp.einsum("brd,bcr->bdc", p_lo, q_lo, preferred_element_type=F32)
    new_errors = (merged.astype(F32) - approx).astype(BF16)[None]
    own_rows = momentum.shape[1]
    mine = lax.dynamic_slice_in_dim(approx, lax.axis_index("replica") * own_rows, own_rows, 1)
    return new_errors, 0.9 * momentum + mine, 0.9 * vec_momentum + vec_sum / replicas


def solution(mesh):
    few = mesh.shape["replica"] == 4
    wide = P("replica", "section", None, "tensor")
    outs = (wide, P("section", "replica", "tensor"), P("section", "tensor"))
    return jax.shard_map(
        gathered if few else reduced,
        mesh=mesh,
        in_specs=(wide, wide, P("section", "tensor", None), outs[1], P("replica", "section", "tensor"), outs[2]),
        out_specs=outs,
        check_vma=False,
    )
```

```python
import functools

import jax
import jax.numpy as jnp
from jax import lax
from jax.experimental import pallas as pl
from jax.experimental.pallas import tpu as pltpu
from jax.sharding import PartitionSpec as P

ROUNDS = 2
LANES = 128
PAD = 16
CHUNKS_IN, CHUNKS_OUT = 2, 4
STEP = 16
HIGHEST = lax.Precision.HIGHEST
F32, BF16 = jnp.float32, jnp.bfloat16
VMEM = pl.BlockSpec(memory_space=pltpu.VMEM)
HBM = pl.BlockSpec(memory_space=pltpu.MemorySpace.HBM)


def dot(a, b, ca, cb, precision=None):
    return lax.dot_general(a, b, (((ca,), (cb,)), ((), ())), precision=precision, preferred_element_type=F32)


def call(kernel, outs, *args, flops=0, in_specs=None, out_specs=None, scratch=(), limit=32, cost=None):
    size = sum(a.size * a.dtype.itemsize for a in (*args, *outs))
    return pl.pallas_call(
        kernel,
        out_shape=outs,
        in_specs=in_specs or [VMEM] * len(args),
        out_specs=out_specs or [VMEM] * len(outs),
        scratch_shapes=scratch,
        compiler_params=pltpu.CompilerParams(vmem_limit_bytes=limit * 1024 * 1024),
        cost_estimate=pl.CostEstimate(flops=flops, bytes_accessed=cost or size, transcendentals=0),
    )(*args)


def three_parts(x):
    hi = x.astype(BF16).astype(F32)
    mid = (x - hi).astype(BF16).astype(F32)
    lo = (x - hi - mid).astype(BF16).astype(F32)
    return hi, mid, lo


def tree(values):
    values = list(values)
    while len(values) > 1:
        values = [a + b for a, b in zip(values[::2], values[1::2])] + values[len(values) & ~1 :]
    return values[0]


def inverse_factor(gram):
    n = gram.shape[0]
    wide = max(128, 2 * n)
    eye = (lax.broadcasted_iota(jnp.int32, (n, n), 0) == lax.broadcasted_iota(jnp.int32, (n, n), 1)).astype(F32)
    row = lax.broadcasted_iota(jnp.int32, (n, wide), 0)
    both = jnp.concatenate([gram, eye, jnp.zeros((n, wide - 2 * n), F32)], axis=1)
    scale = jnp.zeros((n, wide), F32)
    for first in range(0, n, STEP):
        columns = [jnp.broadcast_to(both[:, k : k + 1], (n, wide)) for k in range(first, first + STEP)]
        for j in range(STEP):
            k = first + j
            inverse = 1.0 / jnp.broadcast_to(columns[j][k : k + 1, :], (n, wide))
            scale = jnp.where(row == k, inverse, scale)
            factor = jnp.where(row > k, columns[j] * inverse, 0.0)
            for i in range(j + 1, STEP):
                columns[i] = columns[i] - factor * columns[i][k : k + 1, :]
            both = both - factor * both[k : k + 1, :]
    return both[:, n : 2 * n] * jnp.sqrt(scale[:, :n])


def merge_kernel(grads, errors, q, vec, merged, p_part, grads_in, errors_in, q_in, vec_in, sems):
    rows, cols = grads.shape
    step = rows // CHUNKS_IN
    small = [pltpu.make_async_copy(a, b, sems.at[2, i]) for i, (a, b) in enumerate([(q, q_in), (vec, vec_in)])]
    large = [
        [
            pltpu.make_async_copy(a.at[pl.ds(i * step, step)], b.at[pl.ds(i * step, step)], sems.at[j, i])
            for j, (a, b) in enumerate([(grads, grads_in), (errors, errors_in)])
        ]
        for i in range(CHUNKS_IN)
    ]
    for copy in small + sum(large, []):
        copy.start()
    for copy in small:
        copy.wait()
    q_lo = q_in[...].astype(BF16)
    parts = three_parts(vec_in[...])
    merged[rows:, :] = jnp.concatenate([*parts, jnp.zeros((PAD - 3, cols), F32)], axis=0).astype(BF16)
    for i in range(CHUNKS_IN):
        for copy in large[i]:
            copy.wait()
        here = slice(i * step, (i + 1) * step)
        total = (grads_in[here, :].astype(F32) + errors_in[here, :].astype(F32)).astype(BF16)
        merged[here, :] = total
        p_part[:, here] = dot(q_lo, total, 1, 1)


def add_kernel(*refs):
    refs[-1][...] = tree([r[...] for r in refs[:-1]])


def own_block(owner):
    return lax.axis_index("replica") == owner[0] + lax.axis_index("section") * (owner[-1] - owner[0])


def factor_kernel(replicas, owner, *refs):
    @pl.when(own_block(owner))
    def _():
        p_sum = tree([p[...] for p in refs[:-1]]) * (1.0 / replicas)
        inverse = inverse_factor(dot(p_sum, p_sum, 1, 1, HIGHEST))
        refs[-1][...] = dot(inverse, p_sum, 1, 0, HIGHEST).astype(BF16)


def product(left, mean, here, axis):
    high, low = mean
    return dot(left, high[here, :], 1, axis) + dot(left, low[here, :], 1, axis)


def turn_kernel(replicas, owner, p_lo, *refs):
    *merged, high, low, vec_mean, out = refs
    rows = high.shape[0]

    @pl.when(own_block(owner))
    def _():
        total = tree([m[:rows, :].astype(F32) for m in merged]) * (1.0 / replicas)
        top = total.astype(BF16)
        high[...] = top
        low[...] = (total - top.astype(F32)).astype(BF16)
        vec_mean[...] = tree([jnp.sum(m[rows:, :].astype(F32), axis=0, keepdims=True) for m in merged]) * (1.0 / replicas)
        everything = slice(0, rows)
        q_lo = product(p_lo[...], (high, low), everything, 0).astype(BF16)
        out[...] = product(q_lo, (high, low), everything, 1)


def last_kernel(owner, p_lo, high, low, vec_mean, out):
    rows, cols = high.shape

    @pl.when(own_block(owner))
    def _():
        q_lo = product(p_lo[...], (high, low), slice(0, rows), 0).astype(BF16)
        vec = vec_mean[...]
        parts = [part[:, i : i + LANES] for part in three_parts(vec) for i in range(0, cols, LANES)]
        fill = jnp.zeros((out.shape[0] - len(parts), LANES), F32)
        out[:, :rows] = p_lo[...]
        out[:, rows : rows + cols] = q_lo
        out[:, rows + cols :] = jnp.concatenate([*parts, fill], axis=0).astype(BF16)


def final_kernel(sources, merged, momentum, vec_momentum, *refs):
    packs = refs[:-9]
    new_errors, new_momentum, new_vec, rest, p_rows, errors_out, momentum_out, vec_out, sems = refs[-9:]
    rows, cols = new_errors.shape
    own_rows = momentum.shape[0]
    z, s = lax.axis_index("replica"), lax.axis_index("section")
    came = sum(
        jnp.where((z == row[j]) & (s == i), (0, 1, 2)[j] + 1, 0) for i, row in enumerate(sources) for j in range(len(row))
    )
    for i, pack in enumerate(packs):

        @pl.when(came == i)
        def _(pack=pack):
            p_rows[...] = pack[:, :rows].T
            rest[...] = pack[:, rows:]

    q_lo = rest[:, :cols]
    copies = []
    step = rows // CHUNKS_OUT
    for i in range(CHUNKS_OUT):
        here = pl.ds(i * step, step)
        approx = dot(p_rows[here, :], q_lo, 1, 0)
        errors_out[here, :] = (merged[here, :].astype(F32) - approx).astype(BF16)
        copies.append(pltpu.make_async_copy(errors_out.at[here], new_errors.at[here], sems.at[i]))
        copies[-1].start()
    start = pl.multiple_of(z * own_rows, own_rows)
    mine = dot(p_rows[pl.ds(start, own_rows), :], q_lo, 1, 0)
    momentum_out[...] = 0.9 * momentum[...] + mine
    copies.append(pltpu.make_async_copy(momentum_out, new_momentum, sems.at[CHUNKS_OUT]))
    copies[-1].start()
    parts = rest[:, cols:].astype(F32)
    pieces = cols // LANES
    for i in range(pieces):
        vec = parts[i : i + 1] + parts[pieces + i : pieces + i + 1] + parts[2 * pieces + i : 2 * pieces + i + 1]
        here = slice(i * LANES, (i + 1) * LANES)
        vec_out[:, here] = 0.9 * vec_momentum[:, here] + vec
    copies.append(pltpu.make_async_copy(vec_out, new_vec, sems.at[CHUNKS_OUT + 1]))
    copies[-1].start()
    for copy in copies:
        copy.wait()


def completed(needed, places):
    needed = list(needed)
    sources = [p for p in places if p not in [a for a, _ in needed]]
    targets = [p for p in places if p not in [b for _, b in needed]]
    far = {(a, b): (a == b, 2 * abs(a[0] - b[0]) + (a[1] != b[1]), a, b) for a in sources for b in targets}
    for a, b in sorted(far, key=far.get):
        if a in sources and b in targets:
            sources.remove(a)
            targets.remove(b)
            needed.append((a, b))
    return needed


def gathered(grads, errors, q_start, momentum, vec_grads, vec_momentum):
    replicas, tensors, sections = (lax.axis_size(a) for a in ("replica", "tensor", "section"))
    rows, cols = grads.shape[2:]
    rank = q_start.shape[2]
    middle = (replicas - 1) // 2
    distance = lambda z, o: (-(abs(2 * z - replicas + 1) <= 1), -abs(z - o))
    owner = [middle + s % min(2, replicas) for s in range(sections)]
    sources = [sorted((z for z in range(replicas) if z != o), key=lambda z, o=o: distance(z, o)) for o in owner]
    places = [(z, s) for z in range(replicas) for s in range(sections)]
    inward = [
        completed([((sources[s][j], s), (owner[s], s)) for s in range(sections)], places) for j in range(replicas - 1)
    ]
    outward = [[(b, a) for a, b in pairs] for pairs in inward]
    number = lambda place: place[0] * sections + place[1]

    def along(x, perms):
        return [lax.ppermute(x, ("replica", "section"), [(number(a), number(b)) for a, b in p]) for p in perms]

    def across(x, steps, busy):
        parts = [x]
        for k in steps:
            idle = [p for p in places if p not in busy]
            pairs = [((z, i, s), (z, i ^ k, s)) for z, s in busy for i in range(tensors)]
            pairs += [((a[0], i, a[1]), (b[0], i, b[1])) for a, b in completed([], idle) for i in range(tensors)]
            order = [((a[0] * tensors + a[1]) * sections + a[2], (b[0] * tensors + b[1]) * sections + b[2]) for a, b in pairs]
            parts.append(lax.ppermute(x, ("replica", "tensor", "section"), order))
        return parts

    p_shape = jax.ShapeDtypeStruct((rank, rows), F32)
    work = 2 * rows * cols * rank
    block = (rows, cols)
    merged_shape = jax.ShapeDtypeStruct((rows + PAD, cols), BF16)
    merged, p_part = call(
        merge_kernel,
        [merged_shape, p_shape],
        *(pltpu.with_memory_space_constraint(x, pltpu.HBM) for x in (grads[0, 0], errors[0, 0], q_start[0].T, vec_grads[0])),
        flops=work,
        in_specs=[HBM] * 4,
        scratch=[
            pltpu.VMEM(block, BF16),
            pltpu.VMEM(block, BF16),
            pltpu.VMEM((rank, cols), F32),
            pltpu.VMEM((1, cols), F32),
            pltpu.SemaphoreType.DMA((3, CHUNKS_IN)),
        ],
    )
    planes = [p for p in places if p[0] in owner]
    p_in = along(p_part, inward)
    m_near = along(merged, inward[:1] + inward[2:])
    p_part = call(add_kernel, [p_shape], p_part, *(p_in[i] for i in (2, 0, 1)))[0]
    held = lax.optimization_barrier((merged, p_part))[0]
    m_in = along(held, inward[1:2]) + m_near
    k = 1
    while 2 * k < tensors:
        p_part = tree(across(p_part, [k], planes))
        k *= 2
    parts = across(p_part, [k] if k < tensors else [], planes)
    lo_shape = jax.ShapeDtypeStruct((rank, rows), BF16)
    for _ in range(ROUNDS - 1):
        p_lo = call(functools.partial(factor_kernel, replicas, owner), [lo_shape], *parts)[0]
        *mean, p_part = call(
            functools.partial(turn_kernel, replicas, owner),
            [jax.ShapeDtypeStruct(block, BF16)] * 2 + [jax.ShapeDtypeStruct((1, cols), F32), p_shape],
            p_lo,
            merged,
            *(m_in[i] for i in (1, 2, 0)),
            flops=4 * work,
        )
        parts = across(p_part, range(1, tensors), [(owner[s], s) for s in range(sections)])
    p_lo = call(functools.partial(factor_kernel, replicas, owner), [lo_shape], *parts)[0]
    whole = call(
        functools.partial(last_kernel, owner),
        [jax.ShapeDtypeStruct((rank, rows + cols + LANES), BF16)],
        p_lo,
        *mean,
        flops=2 * work,
    )[0]
    received = along(whole, outward)
    new_errors, new_momentum, new_vec = call(
        functools.partial(final_kernel, sources),
        [
            jax.ShapeDtypeStruct(block, BF16),
            jax.ShapeDtypeStruct(momentum.shape[1:], F32),
            jax.ShapeDtypeStruct((1, cols), F32),
        ],
        merged,
        momentum[0],
        vec_momentum,
        whole,
        *(received[i] for i in (0, 1, 2)),
        flops=2 * work,
        out_specs=[HBM] * 3,
        scratch=[
            pltpu.VMEM((rank, cols + LANES), BF16),
            pltpu.VMEM((rows, rank), BF16),
            pltpu.VMEM(block, BF16),
            pltpu.VMEM(momentum.shape[1:], F32),
            pltpu.VMEM((1, cols), F32),
            pltpu.SemaphoreType.DMA((CHUNKS_OUT + 2,)),
        ],
    )
    return new_errors[None, None], new_momentum[None], new_vec


def reduced(grads, errors, q_start, momentum, vec_grads, vec_momentum):
    replicas = lax.axis_size("replica")
    merged = (grads[0].astype(F32) + errors[0].astype(F32)).astype(BF16)
    q_lo = q_start.astype(BF16)
    vec_sum = lax.psum(vec_grads[0], "replica")
    p_lo = None
    for _ in range(ROUNDS):
        p_part = jnp.einsum("bdc,bcr->brd", merged, q_lo, preferred_element_type=F32)
        p_sum = lax.psum(p_part, ("replica", "tensor")) / replicas
        gram = jnp.einsum("brd,bsd->brs", p_sum, p_sum, precision=HIGHEST)
        inverse = jnp.stack([inverse_factor(g) for g in gram])
        p_lo = jnp.einsum("brs,bsd->brd", inverse, p_sum, precision=HIGHEST).astype(BF16)
        q_part = jnp.einsum("bdc,brd->bcr", merged, p_lo, preferred_element_type=F32)
        q_lo = (lax.psum(q_part, "replica") / replicas).astype(BF16)
    approx = jnp.einsum("brd,bcr->bdc", p_lo, q_lo, preferred_element_type=F32)
    new_errors = (merged.astype(F32) - approx).astype(BF16)[None]
    own_rows = momentum.shape[1]
    mine = lax.dynamic_slice_in_dim(approx, lax.axis_index("replica") * own_rows, own_rows, 1)
    return new_errors, 0.9 * momentum + mine, 0.9 * vec_momentum + vec_sum / replicas


def solution(mesh):
    few = mesh.shape["replica"] == 4
    wide = P("replica", "section", None, "tensor")
    outs = (wide, P("section", "replica", "tensor"), P("section", "tensor"))
    return jax.shard_map(
        gathered if few else reduced,
        mesh=mesh,
        in_specs=(wide, wide, P("section", "tensor", None), outs[1], P("replica", "section", "tensor"), outs[2]),
        out_specs=outs,
        check_vma=False,
    )
```

```python
import functools

import jax
import jax.numpy as jnp
from jax import lax
from jax.experimental import pallas as pl
from jax.experimental.pallas import tpu as pltpu
from jax.sharding import PartitionSpec as P

ROUNDS = 2
LANES = 128
PAD = 16
CHUNKS_IN, CHUNKS_OUT = 2, 4
STEP = 16
HIGHEST = lax.Precision.HIGHEST
F32, BF16 = jnp.float32, jnp.bfloat16
VMEM = pl.BlockSpec(memory_space=pltpu.VMEM)
HBM = pl.BlockSpec(memory_space=pltpu.MemorySpace.HBM)


def dot(a, b, ca, cb, precision=None):
    return lax.dot_general(a, b, (((ca,), (cb,)), ((), ())), precision=precision, preferred_element_type=F32)


def call(kernel, outs, *args, flops=0, in_specs=None, out_specs=None, scratch=(), limit=32, cost=None):
    size = sum(a.size * a.dtype.itemsize for a in (*args, *outs))
    return pl.pallas_call(
        kernel,
        out_shape=outs,
        in_specs=in_specs or [VMEM] * len(args),
        out_specs=out_specs or [VMEM] * len(outs),
        scratch_shapes=scratch,
        compiler_params=pltpu.CompilerParams(vmem_limit_bytes=limit * 1024 * 1024),
        cost_estimate=pl.CostEstimate(flops=flops, bytes_accessed=cost or size, transcendentals=0),
    )(*args)


def three_parts(x):
    hi = x.astype(BF16).astype(F32)
    mid = (x - hi).astype(BF16).astype(F32)
    lo = (x - hi - mid).astype(BF16).astype(F32)
    return hi, mid, lo


def tree(values):
    values = list(values)
    while len(values) > 1:
        values = [a + b for a, b in zip(values[::2], values[1::2])] + values[len(values) & ~1 :]
    return values[0]


def inverse_factor(gram):
    n = gram.shape[0]
    wide = max(128, 2 * n)
    eye = (lax.broadcasted_iota(jnp.int32, (n, n), 0) == lax.broadcasted_iota(jnp.int32, (n, n), 1)).astype(F32)
    row = lax.broadcasted_iota(jnp.int32, (n, wide), 0)
    both = jnp.concatenate([gram, eye, jnp.zeros((n, wide - 2 * n), F32)], axis=1)
    scale = jnp.zeros((n, wide), F32)
    for first in range(0, n, STEP):
        columns = [jnp.broadcast_to(both[:, k : k + 1], (n, wide)) for k in range(first, first + STEP)]
        for j in range(STEP):
            k = first + j
            inverse = 1.0 / jnp.broadcast_to(columns[j][k : k + 1, :], (n, wide))
            scale = jnp.where(row == k, inverse, scale)
            factor = jnp.where(row > k, columns[j] * inverse, 0.0)
            for i in range(j + 1, STEP):
                columns[i] = columns[i] - factor * columns[i][k : k + 1, :]
            both = both - factor * both[k : k + 1, :]
    return both[:, n : 2 * n] * jnp.sqrt(scale[:, :n])


def merge_kernel(grads, errors, q, vec, merged, p_part, grads_in, errors_in, q_in, vec_in, sems):
    rows, cols = grads.shape
    step = rows // CHUNKS_IN
    small = [pltpu.make_async_copy(a, b, sems.at[2, i]) for i, (a, b) in enumerate([(q, q_in), (vec, vec_in)])]
    large = [
        [
            pltpu.make_async_copy(a.at[pl.ds(i * step, step)], b.at[pl.ds(i * step, step)], sems.at[j, i])
            for j, (a, b) in enumerate([(grads, grads_in), (errors, errors_in)])
        ]
        for i in range(CHUNKS_IN)
    ]
    for copy in small + sum(large, []):
        copy.start()
    for copy in small:
        copy.wait()
    q_lo = q_in[...].astype(BF16)
    parts = three_parts(vec_in[...])
    merged[rows:, :] = jnp.concatenate([*parts, jnp.zeros((PAD - 3, cols), F32)], axis=0).astype(BF16)
    for i in range(CHUNKS_IN):
        for copy in large[i]:
            copy.wait()
        here = slice(i * step, (i + 1) * step)
        total = (grads_in[here, :].astype(F32) + errors_in[here, :].astype(F32)).astype(BF16)
        merged[here, :] = total
        p_part[:, here] = dot(q_lo, total, 1, 1)


def add_kernel(*refs):
    refs[-1][...] = tree([r[...] for r in refs[:-1]])


def own_block(owner):
    return lax.axis_index("replica") == owner[0] + lax.axis_index("section") * (owner[-1] - owner[0])


def factor_kernel(replicas, owner, *refs):
    @pl.when(own_block(owner))
    def _():
        p_sum = tree([p[...] for p in refs[:-1]]) * (1.0 / replicas)
        inverse = inverse_factor(dot(p_sum, p_sum, 1, 1, HIGHEST))
        refs[-1][...] = dot(inverse, p_sum, 1, 0, HIGHEST).astype(BF16)


def product(left, mean, here, axis):
    high, low = mean
    return dot(left, high[here, :], 1, axis) + dot(left, low[here, :], 1, axis)


def turn_kernel(replicas, owner, p_lo, *refs):
    *merged, high, low, vec_mean, out = refs
    rows = high.shape[0]

    @pl.when(own_block(owner))
    def _():
        total = tree([m[:rows, :].astype(F32) for m in merged]) * (1.0 / replicas)
        top = total.astype(BF16)
        high[...] = top
        low[...] = (total - top.astype(F32)).astype(BF16)
        vec_mean[...] = tree([jnp.sum(m[rows:, :].astype(F32), axis=0, keepdims=True) for m in merged]) * (1.0 / replicas)
        everything = slice(0, rows)
        q_lo = product(p_lo[...], (high, low), everything, 0).astype(BF16)
        out[...] = product(q_lo, (high, low), everything, 1)


def last_kernel(owner, p_lo, high, low, vec_mean, out):
    rows, cols = high.shape

    @pl.when(own_block(owner))
    def _():
        q_lo = product(p_lo[...], (high, low), slice(0, rows), 0).astype(BF16)
        vec = vec_mean[...]
        parts = [part[:, i : i + LANES] for part in three_parts(vec) for i in range(0, cols, LANES)]
        fill = jnp.zeros((out.shape[0] - len(parts), LANES), F32)
        out[:, :rows] = p_lo[...]
        out[:, rows : rows + cols] = q_lo
        out[:, rows + cols :] = jnp.concatenate([*parts, fill], axis=0).astype(BF16)


def final_kernel(sources, merged, momentum, vec_momentum, *refs):
    packs = refs[:-9]
    new_errors, new_momentum, new_vec, rest, p_rows, errors_out, momentum_out, vec_out, sems = refs[-9:]
    rows, cols = new_errors.shape
    own_rows = momentum.shape[0]
    z, s = lax.axis_index("replica"), lax.axis_index("section")
    came = sum(
        jnp.where((z == row[j]) & (s == i), (0, 1, 2)[j] + 1, 0) for i, row in enumerate(sources) for j in range(len(row))
    )
    for i, pack in enumerate(packs):

        @pl.when(came == i)
        def _(pack=pack):
            p_rows[...] = pack[:, :rows].T
            rest[...] = pack[:, rows:]

    q_lo = rest[:, :cols]
    copies = []
    step = rows // CHUNKS_OUT
    for i in range(CHUNKS_OUT):
        here = pl.ds(i * step, step)
        approx = dot(p_rows[here, :], q_lo, 1, 0)
        errors_out[here, :] = (merged[here, :].astype(F32) - approx).astype(BF16)
        copies.append(pltpu.make_async_copy(errors_out.at[here], new_errors.at[here], sems.at[i]))
        copies[-1].start()
    start = pl.multiple_of(z * own_rows, own_rows)
    mine = dot(p_rows[pl.ds(start, own_rows), :], q_lo, 1, 0)
    momentum_out[...] = 0.9 * momentum[...] + mine
    copies.append(pltpu.make_async_copy(momentum_out, new_momentum, sems.at[CHUNKS_OUT]))
    copies[-1].start()
    parts = rest[:, cols:].astype(F32)
    pieces = cols // LANES
    for i in range(pieces):
        vec = parts[i : i + 1] + parts[pieces + i : pieces + i + 1] + parts[2 * pieces + i : 2 * pieces + i + 1]
        here = slice(i * LANES, (i + 1) * LANES)
        vec_out[:, here] = 0.9 * vec_momentum[:, here] + vec
    copies.append(pltpu.make_async_copy(vec_out, new_vec, sems.at[CHUNKS_OUT + 1]))
    copies[-1].start()
    for copy in copies:
        copy.wait()


def completed(needed, places):
    needed = list(needed)
    sources = [p for p in places if p not in [a for a, _ in needed]]
    targets = [p for p in places if p not in [b for _, b in needed]]
    far = {(a, b): (a == b, 2 * abs(a[0] - b[0]) + (a[1] != b[1]), a, b) for a in sources for b in targets}
    for a, b in sorted(far, key=far.get):
        if a in sources and b in targets:
            sources.remove(a)
            targets.remove(b)
            needed.append((a, b))
    return needed


def gathered(grads, errors, q_start, momentum, vec_grads, vec_momentum):
    replicas, tensors, sections = (lax.axis_size(a) for a in ("replica", "tensor", "section"))
    rows, cols = grads.shape[2:]
    rank = q_start.shape[2]
    middle = (replicas - 1) // 2
    distance = lambda z, o: (-(abs(2 * z - replicas + 1) <= 1), -abs(z - o))
    owner = [middle + s % min(2, replicas) for s in range(sections)]
    sources = [sorted((z for z in range(replicas) if z != o), key=lambda z, o=o: distance(z, o)) for o in owner]
    places = [(z, s) for z in range(replicas) for s in range(sections)]
    inward = [
        completed([((sources[s][j], s), (owner[s], s)) for s in range(sections)], places) for j in range(replicas - 1)
    ]
    outward = [[(b, a) for a, b in pairs] for pairs in inward]
    number = lambda place: place[0] * sections + place[1]
    device = lambda place: (place[0] * tensors + place[1]) * sections + place[2]

    def along(x, perms):
        return [lax.ppermute(x, ("replica", "section"), [(number(a), number(b)) for a, b in p]) for p in perms]

    def across(x, steps, busy):
        parts = [x]
        for k in steps:
            idle = [p for p in places if p not in busy]
            pairs = [((z, i, s), (z, i ^ k, s)) for z, s in busy for i in range(tensors)]
            pairs += [((a[0], i, a[1]), (b[0], i, b[1])) for a, b in completed([], idle) for i in range(tensors)]
            order = [((a[0] * tensors + a[1]) * sections + a[2], (b[0] * tensors + b[1]) * sections + b[2]) for a, b in pairs]
            parts.append(lax.ppermute(x, ("replica", "tensor", "section"), order))
        return parts

    def to_mates(x):
        parts = []
        for k in range(1, tensors):
            pairs = []
            for s in range(sections):
                mate, outer = sections - 1 - s, sources[s][-1]
                ring = [(owner[s], mate), (outer, s), (outer, mate), (owner[s], s)]
                if k < tensors - 1:
                    rest = [(ring[0], ring[3]), (ring[1], ring[2]), (ring[2], ring[1])]
                else:
                    rest = list(zip(ring, ring[1:]))
                for i in range(tensors):
                    pairs.append(((owner[s], i, s), (owner[s], i ^ k, mate)))
                    pairs += [((a[0], i, a[1]), (b[0], i, b[1])) for a, b in rest]
            parts.append(lax.ppermute(x, ("replica", "tensor", "section"), [(device(a), device(b)) for a, b in pairs]))
        return parts

    p_shape = jax.ShapeDtypeStruct((rank, rows), F32)
    work = 2 * rows * cols * rank
    block = (rows, cols)
    merged_shape = jax.ShapeDtypeStruct((rows + PAD, cols), BF16)
    merged, p_part = call(
        merge_kernel,
        [merged_shape, p_shape],
        *(pltpu.with_memory_space_constraint(x, pltpu.HBM) for x in (grads[0, 0], errors[0, 0], q_start[0].T, vec_grads[0])),
        flops=work,
        in_specs=[HBM] * 4,
        scratch=[
            pltpu.VMEM(block, BF16),
            pltpu.VMEM(block, BF16),
            pltpu.VMEM((rank, cols), F32),
            pltpu.VMEM((1, cols), F32),
            pltpu.SemaphoreType.DMA((3, CHUNKS_IN)),
        ],
    )
    planes = [p for p in places if p[0] in owner]
    p_in = along(p_part, inward)
    m_near = along(merged, inward[:1] + inward[2:])
    p_part = call(add_kernel, [p_shape], p_part, *(p_in[i] for i in (2, 0, 1)))[0]
    held = lax.optimization_barrier((merged, p_part))[0]
    m_in = along(held, inward[1:2]) + m_near
    k = 1
    while 2 * k < tensors:
        p_part = tree(across(p_part, [k], planes))
        k *= 2
    parts = across(p_part, [k] if k < tensors else [], planes)
    lo_shape = jax.ShapeDtypeStruct((rank, rows), BF16)
    for _ in range(ROUNDS - 1):
        p_lo = call(functools.partial(factor_kernel, replicas, owner), [lo_shape], *parts)[0]
        *mean, p_part = call(
            functools.partial(turn_kernel, replicas, owner),
            [jax.ShapeDtypeStruct(block, BF16)] * 2 + [jax.ShapeDtypeStruct((1, cols), F32), p_shape],
            p_lo,
            merged,
            *(m_in[i] for i in (1, 2, 0)),
            flops=4 * work,
        )
        p_other = call(add_kernel, [p_shape], *to_mates(p_part))[0]
        parts = [p_part, lax.ppermute(p_other, "section", [(s, sections - 1 - s) for s in range(sections)])]
    p_lo = call(functools.partial(factor_kernel, replicas, owner), [lo_shape], *parts)[0]
    whole = call(
        functools.partial(last_kernel, owner),
        [jax.ShapeDtypeStruct((rank, rows + cols + LANES), BF16)],
        p_lo,
        *mean,
        flops=2 * work,
    )[0]
    received = along(whole, outward)
    new_errors, new_momentum, new_vec = call(
        functools.partial(final_kernel, sources),
        [
            jax.ShapeDtypeStruct(block, BF16),
            jax.ShapeDtypeStruct(momentum.shape[1:], F32),
            jax.ShapeDtypeStruct((1, cols), F32),
        ],
        merged,
        momentum[0],
        vec_momentum,
        whole,
        *(received[i] for i in (0, 1, 2)),
        flops=2 * work,
        out_specs=[HBM] * 3,
        scratch=[
            pltpu.VMEM((rank, cols + LANES), BF16),
            pltpu.VMEM((rows, rank), BF16),
            pltpu.VMEM(block, BF16),
            pltpu.VMEM(momentum.shape[1:], F32),
            pltpu.VMEM((1, cols), F32),
            pltpu.SemaphoreType.DMA((CHUNKS_OUT + 2,)),
        ],
    )
    return new_errors[None, None], new_momentum[None], new_vec


def reduced(grads, errors, q_start, momentum, vec_grads, vec_momentum):
    replicas = lax.axis_size("replica")
    merged = (grads[0].astype(F32) + errors[0].astype(F32)).astype(BF16)
    q_lo = q_start.astype(BF16)
    vec_sum = lax.psum(vec_grads[0], "replica")
    p_lo = None
    for _ in range(ROUNDS):
        p_part = jnp.einsum("bdc,bcr->brd", merged, q_lo, preferred_element_type=F32)
        p_sum = lax.psum(p_part, ("replica", "tensor")) / replicas
        gram = jnp.einsum("brd,bsd->brs", p_sum, p_sum, precision=HIGHEST)
        inverse = jnp.stack([inverse_factor(g) for g in gram])
        p_lo = jnp.einsum("brs,bsd->brd", inverse, p_sum, precision=HIGHEST).astype(BF16)
        q_part = jnp.einsum("bdc,brd->bcr", merged, p_lo, preferred_element_type=F32)
        q_lo = (lax.psum(q_part, "replica") / replicas).astype(BF16)
    approx = jnp.einsum("brd,bcr->bdc", p_lo, q_lo, preferred_element_type=F32)
    new_errors = (merged.astype(F32) - approx).astype(BF16)[None]
    own_rows = momentum.shape[1]
    mine = lax.dynamic_slice_in_dim(approx, lax.axis_index("replica") * own_rows, own_rows, 1)
    return new_errors, 0.9 * momentum + mine, 0.9 * vec_momentum + vec_sum / replicas


def solution(mesh):
    few = mesh.shape["replica"] == 4
    wide = P("replica", "section", None, "tensor")
    outs = (wide, P("section", "replica", "tensor"), P("section", "tensor"))
    return jax.shard_map(
        gathered if few else reduced,
        mesh=mesh,
        in_specs=(wide, wide, P("section", "tensor", None), outs[1], P("replica", "section", "tensor"), outs[2]),
        out_specs=outs,
        check_vma=False,
    )
```

```python
import functools

import jax
import jax.numpy as jnp
from jax import lax
from jax.experimental import pallas as pl
from jax.experimental.pallas import tpu as pltpu
from jax.sharding import PartitionSpec as P

ROUNDS = 2
LANES = 128
PAD = 16
CHUNKS_IN, CHUNKS_OUT = 2, 4
STEP = 16
HIGHEST = lax.Precision.HIGHEST
F32, BF16 = jnp.float32, jnp.bfloat16
VMEM = pl.BlockSpec(memory_space=pltpu.VMEM)
HBM = pl.BlockSpec(memory_space=pltpu.MemorySpace.HBM)


def dot(a, b, ca, cb, precision=None):
    return lax.dot_general(a, b, (((ca,), (cb,)), ((), ())), precision=precision, preferred_element_type=F32)


def call(kernel, outs, *args, flops=0, in_specs=None, out_specs=None, scratch=(), limit=32, cost=None):
    size = sum(a.size * a.dtype.itemsize for a in (*args, *outs))
    return pl.pallas_call(
        kernel,
        out_shape=outs,
        in_specs=in_specs or [VMEM] * len(args),
        out_specs=out_specs or [VMEM] * len(outs),
        scratch_shapes=scratch,
        compiler_params=pltpu.CompilerParams(vmem_limit_bytes=limit * 1024 * 1024),
        cost_estimate=pl.CostEstimate(flops=flops, bytes_accessed=cost or size, transcendentals=0),
    )(*args)


def three_parts(x):
    hi = x.astype(BF16).astype(F32)
    mid = (x - hi).astype(BF16).astype(F32)
    lo = (x - hi - mid).astype(BF16).astype(F32)
    return hi, mid, lo


def tree(values):
    values = list(values)
    while len(values) > 1:
        values = [a + b for a, b in zip(values[::2], values[1::2])] + values[len(values) & ~1 :]
    return values[0]


def inverse_factor(gram):
    n = gram.shape[0]
    wide = max(128, 2 * n)
    eye = (lax.broadcasted_iota(jnp.int32, (n, n), 0) == lax.broadcasted_iota(jnp.int32, (n, n), 1)).astype(F32)
    row = lax.broadcasted_iota(jnp.int32, (n, wide), 0)
    both = jnp.concatenate([gram, eye, jnp.zeros((n, wide - 2 * n), F32)], axis=1)
    scale = jnp.zeros((n, wide), F32)
    for first in range(0, n, STEP):
        columns = [jnp.broadcast_to(both[:, k : k + 1], (n, wide)) for k in range(first, first + STEP)]
        for j in range(STEP):
            k = first + j
            inverse = 1.0 / jnp.broadcast_to(columns[j][k : k + 1, :], (n, wide))
            scale = jnp.where(row == k, inverse, scale)
            factor = jnp.where(row > k, columns[j] * inverse, 0.0)
            for i in range(j + 1, STEP):
                columns[i] = columns[i] - factor * columns[i][k : k + 1, :]
            both = both - factor * both[k : k + 1, :]
    return both[:, n : 2 * n] * jnp.sqrt(scale[:, :n])


def merge_kernel(grads, errors, q, vec, merged, p_part, grads_in, errors_in, q_in, vec_in, sems):
    rows, cols = grads.shape
    step = rows // CHUNKS_IN
    small = [pltpu.make_async_copy(a, b, sems.at[2, i]) for i, (a, b) in enumerate([(q, q_in), (vec, vec_in)])]
    large = [
        [
            pltpu.make_async_copy(a.at[pl.ds(i * step, step)], b.at[pl.ds(i * step, step)], sems.at[j, i])
            for j, (a, b) in enumerate([(grads, grads_in), (errors, errors_in)])
        ]
        for i in range(CHUNKS_IN)
    ]
    for copy in large[0] + small + sum(large[1:], []):
        copy.start()
    for copy in small:
        copy.wait()
    q_lo = q_in[...].astype(BF16)
    for i in range(CHUNKS_IN):
        for copy in large[i]:
            copy.wait()
        here = slice(i * step, (i + 1) * step)
        total = (grads_in[here, :].astype(F32) + errors_in[here, :].astype(F32)).astype(BF16)
        merged[here, :] = total
        p_part[:, here] = dot(q_lo, total, 1, 1)
    parts = three_parts(vec_in[...])
    merged[rows:, :] = jnp.concatenate([*parts, jnp.zeros((PAD - 3, cols), F32)], axis=0).astype(BF16)


def add_kernel(*refs):
    refs[-1][...] = tree([r[...] for r in refs[:-1]])


def own_block(owner):
    return lax.axis_index("replica") == owner[0] + lax.axis_index("section") * (owner[-1] - owner[0])


def factor_kernel(replicas, owner, *refs):
    @pl.when(own_block(owner))
    def _():
        p_sum = tree([p[...] for p in refs[:-1]]) * (1.0 / replicas)
        inverse = inverse_factor(dot(p_sum, p_sum, 1, 1, HIGHEST))
        refs[-1][...] = dot(inverse, p_sum, 1, 0, HIGHEST).astype(BF16)


def product(left, mean, here, axis):
    high, low = mean
    return dot(left, high[here, :], 1, axis) + dot(left, low[here, :], 1, axis)


def turn_kernel(replicas, owner, p_lo, *refs):
    *merged, high, low, vec_mean, out = refs
    rows = high.shape[0]

    @pl.when(own_block(owner))
    def _():
        total = tree([m[:rows, :].astype(F32) for m in merged]) * (1.0 / replicas)
        top = total.astype(BF16)
        high[...] = top
        low[...] = (total - top.astype(F32)).astype(BF16)
        vec_mean[...] = tree([jnp.sum(m[rows:, :].astype(F32), axis=0, keepdims=True) for m in merged]) * (1.0 / replicas)
        everything = slice(0, rows)
        q_lo = product(p_lo[...], (high, low), everything, 0).astype(BF16)
        out[...] = product(q_lo, (high, low), everything, 1)


def last_kernel(owner, p_lo, high, low, vec_mean, out):
    rows, cols = high.shape

    @pl.when(own_block(owner))
    def _():
        q_lo = product(p_lo[...], (high, low), slice(0, rows), 0).astype(BF16)
        vec = vec_mean[...]
        parts = [part[:, i : i + LANES] for part in three_parts(vec) for i in range(0, cols, LANES)]
        fill = jnp.zeros((out.shape[0] - len(parts), LANES), F32)
        out[:, :rows] = p_lo[...]
        out[:, rows : rows + cols] = q_lo
        out[:, rows + cols :] = jnp.concatenate([*parts, fill], axis=0).astype(BF16)


def final_kernel(sources, merged, momentum, vec_momentum, *refs):
    packs = refs[:-10]
    new_errors, new_momentum, new_vec, rest, left, p_rows, errors_out, momentum_out, vec_out, sems = refs[-10:]
    rows, cols = new_errors.shape
    own_rows = momentum.shape[0]
    z, s = lax.axis_index("replica"), lax.axis_index("section")
    came = sum(
        jnp.where((z == row[j]) & (s == i), (0, 2, 1)[j] + 1, 0) for i, row in enumerate(sources) for j in range(len(row))
    )
    for i, pack in enumerate(packs):

        @pl.when(came == i)
        def _(pack=pack):
            left[...] = pack[:, :rows]
            rest[...] = pack[:, rows:]

    q_lo = rest[:, :cols]
    copies = []
    step = rows // CHUNKS_OUT
    for i in range(CHUNKS_OUT):
        here = pl.ds(i * step, step)
        p_rows[here, :] = left[:, i * step : (i + 1) * step].T
        approx = dot(p_rows[here, :], q_lo, 1, 0)
        errors_out[here, :] = (merged[here, :].astype(F32) - approx).astype(BF16)
        copies.append(pltpu.make_async_copy(errors_out.at[here], new_errors.at[here], sems.at[i]))
        copies[-1].start()
    start = pl.multiple_of(z * own_rows, own_rows)
    mine = dot(p_rows[pl.ds(start, own_rows), :], q_lo, 1, 0)
    momentum_out[...] = 0.9 * momentum[...] + mine
    copies.append(pltpu.make_async_copy(momentum_out, new_momentum, sems.at[CHUNKS_OUT]))
    copies[-1].start()
    parts = rest[:, cols:].astype(F32)
    pieces = cols // LANES
    for i in range(pieces):
        vec = parts[i : i + 1] + parts[pieces + i : pieces + i + 1] + parts[2 * pieces + i : 2 * pieces + i + 1]
        here = slice(i * LANES, (i + 1) * LANES)
        vec_out[:, here] = 0.9 * vec_momentum[:, here] + vec
    copies.append(pltpu.make_async_copy(vec_out, new_vec, sems.at[CHUNKS_OUT + 1]))
    copies[-1].start()
    for copy in copies:
        copy.wait()


def completed(needed, places):
    needed = list(needed)
    sources = [p for p in places if p not in [a for a, _ in needed]]
    targets = [p for p in places if p not in [b for _, b in needed]]
    far = {(a, b): (a == b, 2 * abs(a[0] - b[0]) + (a[1] != b[1]), a, b) for a in sources for b in targets}
    for a, b in sorted(far, key=far.get):
        if a in sources and b in targets:
            sources.remove(a)
            targets.remove(b)
            needed.append((a, b))
    return needed


def gathered(grads, errors, q_start, momentum, vec_grads, vec_momentum):
    replicas, tensors, sections = (lax.axis_size(a) for a in ("replica", "tensor", "section"))
    rows, cols = grads.shape[2:]
    rank = q_start.shape[2]
    middle = (replicas - 1) // 2
    distance = lambda z, o: (-(abs(2 * z - replicas + 1) <= 1), -abs(z - o))
    owner = [middle + s % min(2, replicas) for s in range(sections)]
    sources = [sorted((z for z in range(replicas) if z != o), key=lambda z, o=o: distance(z, o)) for o in owner]
    places = [(z, s) for z in range(replicas) for s in range(sections)]
    inward = [
        completed([((sources[s][j], s), (owner[s], s)) for s in range(sections)], places) for j in range(replicas - 1)
    ]
    outward = [[(b, a) for a, b in pairs] for pairs in inward]
    number = lambda place: place[0] * sections + place[1]
    device = lambda place: (place[0] * tensors + place[1]) * sections + place[2]

    def along(x, perms):
        return [lax.ppermute(x, ("replica", "section"), [(number(a), number(b)) for a, b in p]) for p in perms]

    def across(x, steps, busy):
        parts = [x]
        for k in steps:
            idle = [p for p in places if p not in busy]
            pairs = [((z, i, s), (z, i ^ k, s)) for z, s in busy for i in range(tensors)]
            pairs += [((a[0], i, a[1]), (b[0], i, b[1])) for a, b in completed([], idle) for i in range(tensors)]
            order = [((a[0] * tensors + a[1]) * sections + a[2], (b[0] * tensors + b[1]) * sections + b[2]) for a, b in pairs]
            parts.append(lax.ppermute(x, ("replica", "tensor", "section"), order))
        return parts

    def to_mates(x):
        parts = []
        for k in range(1, tensors):
            pairs = []
            for s in range(sections):
                mate, outer = sections - 1 - s, sources[s][-1]
                ring = [(owner[s], mate), (outer, s), (outer, mate), (owner[s], s)]
                if k < tensors - 1:
                    rest = [(ring[0], ring[3]), (ring[1], ring[2]), (ring[2], ring[1])]
                else:
                    rest = list(zip(ring, ring[1:]))
                for i in range(tensors):
                    pairs.append(((owner[s], i, s), (owner[s], i ^ k, mate)))
                    pairs += [((a[0], i, a[1]), (b[0], i, b[1])) for a, b in rest]
            parts.append(lax.ppermute(x, ("replica", "tensor", "section"), [(device(a), device(b)) for a, b in pairs]))
        return parts

    p_shape = jax.ShapeDtypeStruct((rank, rows), F32)
    work = 2 * rows * cols * rank
    block = (rows, cols)
    merged_shape = jax.ShapeDtypeStruct((rows + PAD, cols), BF16)
    merged, p_part = call(
        merge_kernel,
        [merged_shape, p_shape],
        *(pltpu.with_memory_space_constraint(x, pltpu.HBM) for x in (grads[0, 0], errors[0, 0], q_start[0].T, vec_grads[0])),
        flops=work,
        in_specs=[HBM] * 4,
        scratch=[
            pltpu.VMEM(block, BF16),
            pltpu.VMEM(block, BF16),
            pltpu.VMEM((rank, cols), F32),
            pltpu.VMEM((1, cols), F32),
            pltpu.SemaphoreType.DMA((3, CHUNKS_IN)),
        ],
    )
    planes = [p for p in places if p[0] in owner]
    p_in = along(p_part, inward)
    m_near = along(merged, inward[:1] + inward[2:])
    p_part = call(add_kernel, [p_shape], p_part, *(p_in[i] for i in (2, 0, 1)))[0]
    held = lax.optimization_barrier((merged, p_part))[0]
    m_in = along(held, inward[1:2]) + m_near
    k = 1
    while 2 * k < tensors:
        p_part = tree(across(p_part, [k], planes))
        k *= 2
    parts = across(p_part, [k] if k < tensors else [], planes)
    lo_shape = jax.ShapeDtypeStruct((rank, rows), BF16)
    for _ in range(ROUNDS - 1):
        p_lo = call(functools.partial(factor_kernel, replicas, owner), [lo_shape], *parts)[0]
        *mean, p_part = call(
            functools.partial(turn_kernel, replicas, owner),
            [jax.ShapeDtypeStruct(block, BF16)] * 2 + [jax.ShapeDtypeStruct((1, cols), F32), p_shape],
            p_lo,
            merged,
            *(m_in[i] for i in (1, 2, 0)),
            flops=4 * work,
        )
        p_other = call(add_kernel, [p_shape], *to_mates(p_part))[0]
        parts = [p_part, lax.ppermute(p_other, "section", [(s, sections - 1 - s) for s in range(sections)])]
    p_lo = call(functools.partial(factor_kernel, replicas, owner), [lo_shape], *parts)[0]
    whole = call(
        functools.partial(last_kernel, owner),
        [jax.ShapeDtypeStruct((rank, rows + cols + LANES), BF16)],
        p_lo,
        *mean,
        flops=2 * work,
    )[0]
    received = along(whole, outward)
    new_errors, new_momentum, new_vec = call(
        functools.partial(final_kernel, sources),
        [
            jax.ShapeDtypeStruct(block, BF16),
            jax.ShapeDtypeStruct(momentum.shape[1:], F32),
            jax.ShapeDtypeStruct((1, cols), F32),
        ],
        merged,
        momentum[0],
        vec_momentum,
        whole,
        *(received[i] for i in (0, 2, 1)),
        flops=2 * work,
        out_specs=[HBM] * 3,
        scratch=[
            pltpu.VMEM((rank, cols + LANES), BF16),
            pltpu.VMEM((rank, rows), BF16),
            pltpu.VMEM((rows, rank), BF16),
            pltpu.VMEM(block, BF16),
            pltpu.VMEM(momentum.shape[1:], F32),
            pltpu.VMEM((1, cols), F32),
            pltpu.SemaphoreType.DMA((CHUNKS_OUT + 2,)),
        ],
    )
    return new_errors[None, None], new_momentum[None], new_vec


def reduced(grads, errors, q_start, momentum, vec_grads, vec_momentum):
    replicas = lax.axis_size("replica")
    merged = (grads[0].astype(F32) + errors[0].astype(F32)).astype(BF16)
    q_lo = q_start.astype(BF16)
    vec_sum = lax.psum(vec_grads[0], "replica")
    p_lo = None
    for _ in range(ROUNDS):
        p_part = jnp.einsum("bdc,bcr->brd", merged, q_lo, preferred_element_type=F32)
        p_sum = lax.psum(p_part, ("replica", "tensor")) / replicas
        gram = jnp.einsum("brd,bsd->brs", p_sum, p_sum, precision=HIGHEST)
        inverse = jnp.stack([inverse_factor(g) for g in gram])
        p_lo = jnp.einsum("brs,bsd->brd", inverse, p_sum, precision=HIGHEST).astype(BF16)
        q_part = jnp.einsum("bdc,brd->bcr", merged, p_lo, preferred_element_type=F32)
        q_lo = (lax.psum(q_part, "replica") / replicas).astype(BF16)
    approx = jnp.einsum("brd,bcr->bdc", p_lo, q_lo, preferred_element_type=F32)
    new_errors = (merged.astype(F32) - approx).astype(BF16)[None]
    own_rows = momentum.shape[1]
    mine = lax.dynamic_slice_in_dim(approx, lax.axis_index("replica") * own_rows, own_rows, 1)
    return new_errors, 0.9 * momentum + mine, 0.9 * vec_momentum + vec_sum / replicas


def solution(mesh):
    few = mesh.shape["replica"] == 4
    wide = P("replica", "section", None, "tensor")
    outs = (wide, P("section", "replica", "tensor"), P("section", "tensor"))
    return jax.shard_map(
        gathered if few else reduced,
        mesh=mesh,
        in_specs=(wide, wide, P("section", "tensor", None), outs[1], P("replica", "section", "tensor"), outs[2]),
        out_specs=outs,
        check_vma=False,
    )
```

```python
import functools

import jax
import jax.numpy as jnp
from jax import lax
from jax.experimental import pallas as pl
from jax.experimental.pallas import tpu as pltpu
from jax.sharding import PartitionSpec as P

ROUNDS = 2
LANES = 128
PAD = 16
CHUNKS_IN, CHUNKS_OUT = 2, 4
STEP = 16
HIGHEST = lax.Precision.HIGHEST
F32, BF16 = jnp.float32, jnp.bfloat16
VMEM = pl.BlockSpec(memory_space=pltpu.VMEM)
HBM = pl.BlockSpec(memory_space=pltpu.MemorySpace.HBM)


def dot(a, b, ca, cb, precision=None):
    return lax.dot_general(a, b, (((ca,), (cb,)), ((), ())), precision=precision, preferred_element_type=F32)


def call(kernel, outs, *args, flops=0, in_specs=None, out_specs=None, scratch=(), limit=32, cost=None):
    size = sum(a.size * a.dtype.itemsize for a in (*args, *outs))
    return pl.pallas_call(
        kernel,
        out_shape=outs,
        in_specs=in_specs or [VMEM] * len(args),
        out_specs=out_specs or [VMEM] * len(outs),
        scratch_shapes=scratch,
        compiler_params=pltpu.CompilerParams(vmem_limit_bytes=limit * 1024 * 1024),
        cost_estimate=pl.CostEstimate(flops=flops, bytes_accessed=cost or size, transcendentals=0),
    )(*args)


def three_parts(x):
    hi = x.astype(BF16).astype(F32)
    mid = (x - hi).astype(BF16).astype(F32)
    lo = (x - hi - mid).astype(BF16).astype(F32)
    return hi, mid, lo


def tree(values):
    values = list(values)
    while len(values) > 1:
        values = [a + b for a, b in zip(values[::2], values[1::2])] + values[len(values) & ~1 :]
    return values[0]


def inverse_factor(gram):
    n = gram.shape[0]
    wide = max(128, 2 * n)
    eye = (lax.broadcasted_iota(jnp.int32, (n, n), 0) == lax.broadcasted_iota(jnp.int32, (n, n), 1)).astype(F32)
    row = lax.broadcasted_iota(jnp.int32, (n, wide), 0)
    both = jnp.concatenate([gram, eye, jnp.zeros((n, wide - 2 * n), F32)], axis=1)
    scale = jnp.zeros((n, wide), F32)
    for first in range(0, n, STEP):
        columns = [jnp.broadcast_to(both[:, k : k + 1], (n, wide)) for k in range(first, first + STEP)]
        for j in range(STEP):
            k = first + j
            inverse = 1.0 / jnp.broadcast_to(columns[j][k : k + 1, :], (n, wide))
            scale = jnp.where(row == k, inverse, scale)
            factor = jnp.where(row > k, columns[j] * inverse, 0.0)
            for i in range(j + 1, STEP):
                columns[i] = columns[i] - factor * columns[i][k : k + 1, :]
            both = both - factor * both[k : k + 1, :]
    return both[:, n : 2 * n] * jnp.sqrt(scale[:, :n])


def merge_kernel(grads, errors, q, vec, merged, p_part, grads_in, errors_in, q_in, vec_in, sems):
    rows, cols = grads.shape
    step = rows // CHUNKS_IN
    small = [pltpu.make_async_copy(a, b, sems.at[2, i]) for i, (a, b) in enumerate([(q, q_in), (vec, vec_in)])]
    large = [
        [
            pltpu.make_async_copy(a.at[pl.ds(i * step, step)], b.at[pl.ds(i * step, step)], sems.at[j, i])
            for j, (a, b) in enumerate([(grads, grads_in), (errors, errors_in)])
        ]
        for i in range(CHUNKS_IN)
    ]
    for copy in large[0] + small + sum(large[1:], []):
        copy.start()
    for copy in small:
        copy.wait()
    q_lo = q_in[...].astype(BF16)
    for i in range(CHUNKS_IN):
        for copy in large[i]:
            copy.wait()
        here = slice(i * step, (i + 1) * step)
        total = (grads_in[here, :].astype(F32) + errors_in[here, :].astype(F32)).astype(BF16)
        merged[here, :] = total
        p_part[:, here] = dot(q_lo, total, 1, 1)
    parts = three_parts(vec_in[...])
    merged[rows:, :] = jnp.concatenate([*parts, jnp.zeros((PAD - 3, cols), F32)], axis=0).astype(BF16)


def add_kernel(*refs):
    refs[-1][...] = tree([r[...] for r in refs[:-1]])


def own_block(owner):
    return lax.axis_index("replica") == owner[0] + lax.axis_index("section") * (owner[-1] - owner[0])


def factor_kernel(replicas, owner, *refs):
    @pl.when(own_block(owner))
    def _():
        p_sum = tree([p[...] for p in refs[:-1]]) * (1.0 / replicas)
        inverse = inverse_factor(dot(p_sum, p_sum, 1, 1, HIGHEST))
        refs[-1][...] = dot(inverse, p_sum, 1, 0, HIGHEST).astype(BF16)


def product(left, mean, here, axis):
    high, low = mean
    return dot(left, high[here, :], 1, axis) + dot(left, low[here, :], 1, axis)


def turn_kernel(replicas, owner, p_lo, *refs):
    *merged, high, low, vec_mean, out = refs
    rows = high.shape[0]

    @pl.when(own_block(owner))
    def _():
        total = tree([m[:rows, :].astype(F32) for m in merged]) * (1.0 / replicas)
        top = total.astype(BF16)
        high[...] = top
        low[...] = (total - top.astype(F32)).astype(BF16)
        vec_mean[...] = tree([jnp.sum(m[rows:, :].astype(F32), axis=0, keepdims=True) for m in merged]) * (1.0 / replicas)
        everything = slice(0, rows)
        q_lo = product(p_lo[...], (high, low), everything, 0).astype(BF16)
        out[...] = product(q_lo, (high, low), everything, 1)


def last_kernel(owner, p_lo, high, low, vec_mean, out):
    rows, cols = high.shape

    @pl.when(own_block(owner))
    def _():
        q_lo = product(p_lo[...], (high, low), slice(0, rows), 0).astype(BF16)
        vec = vec_mean[...]
        parts = [part[:, i : i + LANES] for part in three_parts(vec) for i in range(0, cols, LANES)]
        fill = jnp.zeros((out.shape[0] - len(parts), LANES), F32)
        out[:, :rows] = p_lo[...]
        out[:, rows : rows + cols] = q_lo
        out[:, rows + cols :] = jnp.concatenate([*parts, fill], axis=0).astype(BF16)


def final_kernel(sources, merged, momentum, vec_momentum, *refs):
    packs = refs[:-10]
    new_errors, new_momentum, new_vec, rest, left, p_rows, errors_out, momentum_out, vec_out, sems = refs[-10:]
    rows, cols = new_errors.shape
    own_rows = momentum.shape[0]
    z, s = lax.axis_index("replica"), lax.axis_index("section")
    came = sum(
        jnp.where((z == row[j]) & (s == i), (1, 2, 0)[j] + 1, 0) for i, row in enumerate(sources) for j in range(len(row))
    )
    for i, pack in enumerate(packs):

        @pl.when(came == i)
        def _(pack=pack):
            left[...] = pack[:, :rows]
            rest[...] = pack[:, rows:]

    q_lo = rest[:, :cols]
    copies = []
    step = rows // CHUNKS_OUT
    for i in range(CHUNKS_OUT):
        here = pl.ds(i * step, step)
        p_rows[here, :] = left[:, i * step : (i + 1) * step].T
        approx = dot(p_rows[here, :], q_lo, 1, 0)
        errors_out[here, :] = (merged[here, :].astype(F32) - approx).astype(BF16)
        copies.append(pltpu.make_async_copy(errors_out.at[here], new_errors.at[here], sems.at[i]))
        copies[-1].start()
    start = pl.multiple_of(z * own_rows, own_rows)
    mine = dot(p_rows[pl.ds(start, own_rows), :], q_lo, 1, 0)
    momentum_out[...] = 0.9 * momentum[...] + mine
    copies.append(pltpu.make_async_copy(momentum_out, new_momentum, sems.at[CHUNKS_OUT]))
    copies[-1].start()
    parts = rest[:, cols:].astype(F32)
    pieces = cols // LANES
    for i in range(pieces):
        vec = parts[i : i + 1] + parts[pieces + i : pieces + i + 1] + parts[2 * pieces + i : 2 * pieces + i + 1]
        here = slice(i * LANES, (i + 1) * LANES)
        vec_out[:, here] = 0.9 * vec_momentum[:, here] + vec
    copies.append(pltpu.make_async_copy(vec_out, new_vec, sems.at[CHUNKS_OUT + 1]))
    copies[-1].start()
    for copy in copies:
        copy.wait()


def completed(needed, places):
    needed = list(needed)
    sources = [p for p in places if p not in [a for a, _ in needed]]
    targets = [p for p in places if p not in [b for _, b in needed]]
    far = {(a, b): (a == b, 2 * abs(a[0] - b[0]) + (a[1] != b[1]), a, b) for a in sources for b in targets}
    for a, b in sorted(far, key=far.get):
        if a in sources and b in targets:
            sources.remove(a)
            targets.remove(b)
            needed.append((a, b))
    return needed


def gathered(grads, errors, q_start, momentum, vec_grads, vec_momentum):
    replicas, tensors, sections = (lax.axis_size(a) for a in ("replica", "tensor", "section"))
    rows, cols = grads.shape[2:]
    rank = q_start.shape[2]
    middle = (replicas - 1) // 2
    distance = lambda z, o: (-(abs(2 * z - replicas + 1) <= 1), -abs(z - o))
    owner = [middle + s % min(2, replicas) for s in range(sections)]
    sources = [sorted((z for z in range(replicas) if z != o), key=lambda z, o=o: distance(z, o)) for o in owner]
    places = [(z, s) for z in range(replicas) for s in range(sections)]
    inward = [
        completed([((sources[s][j], s), (owner[s], s)) for s in range(sections)], places) for j in range(replicas - 1)
    ]
    leaving = [[sources[0][0], sources[0][2], sources[0][1]], sources[1]]
    outward = [
        [(b, a) for a, b in completed([((leaving[s][j], s), (owner[s], s)) for s in range(sections)], places)]
        for j in range(replicas - 1)
    ]
    number = lambda place: place[0] * sections + place[1]
    device = lambda place: (place[0] * tensors + place[1]) * sections + place[2]

    def along(x, perms):
        return [lax.ppermute(x, ("replica", "section"), [(number(a), number(b)) for a, b in p]) for p in perms]

    def across(x, steps, busy):
        parts = [x]
        for k in steps:
            idle = [p for p in places if p not in busy]
            pairs = [((z, i, s), (z, i ^ k, s)) for z, s in busy for i in range(tensors)]
            pairs += [((a[0], i, a[1]), (b[0], i, b[1])) for a, b in completed([], idle) for i in range(tensors)]
            order = [((a[0] * tensors + a[1]) * sections + a[2], (b[0] * tensors + b[1]) * sections + b[2]) for a, b in pairs]
            parts.append(lax.ppermute(x, ("replica", "tensor", "section"), order))
        return parts

    def to_mates(x):
        parts = []
        for k in range(1, tensors):
            pairs = []
            for s in range(sections):
                mate, outer = sections - 1 - s, sources[s][-1]
                ring = [(owner[s], mate), (outer, s), (outer, mate), (owner[s], s)]
                if k < tensors - 1:
                    rest = [(ring[0], ring[3]), (ring[1], ring[2]), (ring[2], ring[1])]
                else:
                    rest = list(zip(ring, ring[1:]))
                for i in range(tensors):
                    pairs.append(((owner[s], i, s), (owner[s], i ^ k, mate)))
                    pairs += [((a[0], i, a[1]), (b[0], i, b[1])) for a, b in rest]
            parts.append(lax.ppermute(x, ("replica", "tensor", "section"), [(device(a), device(b)) for a, b in pairs]))
        return parts

    p_shape = jax.ShapeDtypeStruct((rank, rows), F32)
    work = 2 * rows * cols * rank
    block = (rows, cols)
    merged_shape = jax.ShapeDtypeStruct((rows + PAD, cols), BF16)
    merged, p_part = call(
        merge_kernel,
        [merged_shape, p_shape],
        *(pltpu.with_memory_space_constraint(x, pltpu.HBM) for x in (grads[0, 0], errors[0, 0], q_start[0].T, vec_grads[0])),
        flops=work,
        in_specs=[HBM] * 4,
        scratch=[
            pltpu.VMEM(block, BF16),
            pltpu.VMEM(block, BF16),
            pltpu.VMEM((rank, cols), F32),
            pltpu.VMEM((1, cols), F32),
            pltpu.SemaphoreType.DMA((3, CHUNKS_IN)),
        ],
    )
    planes = [p for p in places if p[0] in owner]
    p_in = along(p_part, inward)
    m_near = along(merged, inward[:1] + inward[2:])
    p_part = call(add_kernel, [p_shape], p_part, *(p_in[i] for i in (2, 0, 1)))[0]
    held = lax.optimization_barrier((merged, p_part))[0]
    m_in = along(held, inward[1:2]) + m_near
    k = 1
    while 2 * k < tensors:
        p_part = tree(across(p_part, [k], planes))
        k *= 2
    parts = across(p_part, [k] if k < tensors else [], planes)
    lo_shape = jax.ShapeDtypeStruct((rank, rows), BF16)
    for _ in range(ROUNDS - 1):
        p_lo = call(functools.partial(factor_kernel, replicas, owner), [lo_shape], *parts)[0]
        *mean, p_part = call(
            functools.partial(turn_kernel, replicas, owner),
            [jax.ShapeDtypeStruct(block, BF16)] * 2 + [jax.ShapeDtypeStruct((1, cols), F32), p_shape],
            p_lo,
            merged,
            *(m_in[i] for i in (1, 2, 0)),
            flops=4 * work,
        )
        p_other = call(add_kernel, [p_shape], *to_mates(p_part))[0]
        parts = [p_part, lax.ppermute(p_other, "section", [(s, sections - 1 - s) for s in range(sections)])]
    p_lo = call(functools.partial(factor_kernel, replicas, owner), [lo_shape], *parts)[0]
    whole = call(
        functools.partial(last_kernel, owner),
        [jax.ShapeDtypeStruct((rank, rows + cols + LANES), BF16)],
        p_lo,
        *mean,
        flops=2 * work,
    )[0]
    received = along(whole, outward)
    new_errors, new_momentum, new_vec = call(
        functools.partial(final_kernel, leaving),
        [
            jax.ShapeDtypeStruct(block, BF16),
            jax.ShapeDtypeStruct(momentum.shape[1:], F32),
            jax.ShapeDtypeStruct((1, cols), F32),
        ],
        merged,
        momentum[0],
        vec_momentum,
        whole,
        *(received[i] for i in (2, 0, 1)),
        flops=2 * work,
        out_specs=[HBM] * 3,
        scratch=[
            pltpu.VMEM((rank, cols + LANES), BF16),
            pltpu.VMEM((rank, rows), BF16),
            pltpu.VMEM((rows, rank), BF16),
            pltpu.VMEM(block, BF16),
            pltpu.VMEM(momentum.shape[1:], F32),
            pltpu.VMEM((1, cols), F32),
            pltpu.SemaphoreType.DMA((CHUNKS_OUT + 2,)),
        ],
    )
    return new_errors[None, None], new_momentum[None], new_vec


def reduced(grads, errors, q_start, momentum, vec_grads, vec_momentum):
    replicas = lax.axis_size("replica")
    merged = (grads[0].astype(F32) + errors[0].astype(F32)).astype(BF16)
    q_lo = q_start.astype(BF16)
    vec_sum = lax.psum(vec_grads[0], "replica")
    p_lo = None
    for _ in range(ROUNDS):
        p_part = jnp.einsum("bdc,bcr->brd", merged, q_lo, preferred_element_type=F32)
        p_sum = lax.psum(p_part, ("replica", "tensor")) / replicas
        gram = jnp.einsum("brd,bsd->brs", p_sum, p_sum, precision=HIGHEST)
        inverse = jnp.stack([inverse_factor(g) for g in gram])
        p_lo = jnp.einsum("brs,bsd->brd", inverse, p_sum, precision=HIGHEST).astype(BF16)
        q_part = jnp.einsum("bdc,brd->bcr", merged, p_lo, preferred_element_type=F32)
        q_lo = (lax.psum(q_part, "replica") / replicas).astype(BF16)
    approx = jnp.einsum("brd,bcr->bdc", p_lo, q_lo, preferred_element_type=F32)
    new_errors = (merged.astype(F32) - approx).astype(BF16)[None]
    own_rows = momentum.shape[1]
    mine = lax.dynamic_slice_in_dim(approx, lax.axis_index("replica") * own_rows, own_rows, 1)
    return new_errors, 0.9 * momentum + mine, 0.9 * vec_momentum + vec_sum / replicas


def solution(mesh):
    few = mesh.shape["replica"] == 4
    wide = P("replica", "section", None, "tensor")
    outs = (wide, P("section", "replica", "tensor"), P("section", "tensor"))
    return jax.shard_map(
        gathered if few else reduced,
        mesh=mesh,
        in_specs=(wide, wide, P("section", "tensor", None), outs[1], P("replica", "section", "tensor"), outs[2]),
        out_specs=outs,
        check_vma=False,
    )
```
